32 devices in a mesh: dp: 4 (over y, x), wide: 8 (over z, core).
Axes of the slice: x: 2, y: 2, z: 4, core: 2. Of those that a mesh axis runs over, the one named last changes fastest.
Arguments:
- inputs: float32 [4, 73, 32, 720], P('dp', None, 'wide'), may hold values from -6 to 6
- targets: float32 [4, 73, 32, 720], P('dp', None, 'wide'), may hold values from -6 to 6
- land_mask: int32 [32, 720], P('wide'), may hold values 0 or 1
- missing_mask: int32 [4, 32, 720], P('dp', 'wide'), may hold values from 0 to 1, as said below
- order_map: int32 [360], replicated, may hold values from 0 to 359, each once
- degree_map: int32 [360], replicated, may hold values from 0 to 359, each once
- forward_table: float32 [360, 32, 360], P('wide'), may hold values from -1 to 1
- inverse_table: float32 [360, 360, 32], P('wide'), may hold values from -0.3125 to 0.3125
- spectral_weight: float32 [360, 2, 256, 256], P('wide'), may hold values from -0.25 to 0.25
- spectral_first: float32 [360, 2, 256, 256], P('wide'), may hold values from -8.940697e-08 to 8.940697e-08
- spectral_second: float32 [360, 2, 256, 256], P('wide'), may hold values from 2.10586e-17 to 8.42344e-17
- io_weight: float32 [2, 73, 256], replicated, may hold values from -0.5 to 0.5
- io_first: float32 [2, 73, 256], replicated, may hold values from -8.940697e-08 to 8.940697e-08
- io_second: float32 [2, 73, 256], replicated, may hold values from 2.10586e-17 to 8.42344e-17
- mlp_weight: float32 [2, 256, 512], replicated, may hold values from -0.375 to 0.375
- mlp_first: float32 [2, 256, 512], replicated, may hold values from -8.940697e-08 to 8.940697e-08
- mlp_second: float32 [2, 256, 512], replicated, may hold values from 2.10586e-17 to 8.42344e-17
- biases: float32 [1097], replicated, may hold values from -3 to 3
- bias_first: float32 [1097], replicated, may hold values from -2.9802322e-07 to 2.9802322e-07
- bias_second: float32 [1097], replicated, may hold values from 1.8952741e-16 to 7.5810963e-16
Outputs:
- loss_sum: float32 [], replicated
- valid_weight: float32 [], replicated
- grad_norm: float32 [], replicated
- spectral_new: float32 [360, 2, 256, 256], P('wide')
- spectral_first_new: float32 [360, 2, 256, 256], P('wide')
- spectral_second_new: float32 [360, 2, 256, 256], P('wide')
- spectral_low: bfloat16 [360, 2, 256, 256], P('wide')
- io_new: float32 [2, 73, 256], replicated
- io_first_new: float32 [2, 73, 256], replicated
- io_second_new: float32 [2, 73, 256], replicated
- io_low: bfloat16 [2, 73, 256], replicated
- mlp_new: float32 [2, 256, 512], replicated
- mlp_first_new: float32 [2, 256, 512], replicated
- mlp_second_new: float32 [2, 256, 512], replicated
- mlp_low: bfloat16 [2, 256, 512], replicated
- bias_new: float32 [1097], replicated
- bias_first_new: float32 [1097], replicated
- bias_second_new: float32 [1097], replicated
- bias_low: bfloat16 [1097], replicated
The draws below stay inside these ranges and needn't reach their ends.
Inputs may be any that keep to these rules, and one draw needn't show every extreme that they name: `missing_mask`: 1 marks a missing value. `order_map`: a permutation of 0 to 359; order slot s is held by index s // (360 / size of wide) of the wide axis. `degree_map`: a permutation of 0 to 359; degree slot t is held by index t // (360 / size of wide) of the wide axis.
All inputs are finite; a program needn't handle non-finite values. No bound on the sum of `land_mask` on one device may be relied on, other than what follows from the above.
Results may differ from the reference program's by a relative error of at most 0.001.
Values sent between devices are 32-bit elements; how exact they have to be, the bound alone decides.
No kernel may reach another device: no remote copies, remote signals or barrier semaphores. Data moves between devices by JAX's collectives and lax.ppermute only.
A program may use at most 640 MiB of HBM per device.

```python
import math
import jax
import jax.numpy as jnp
from jax import lax

CH = 73
C = 256
HID = 512
M = 360
L = 360
NLON = 720
SEA_CH = 1
STEP = 5
MS = 360
LS = 360
NLAT = 32
SAMPLES = 4
BIAS = 1097
NPARAM = 47486537


def draw_missing_mask(key, part):
    span = max(SAMPLES - 1, 1)
    latitude = jnp.arange(NLAT, dtype=jnp.int32)[None, :, None]
    sample_index = jnp.arange(SAMPLES, dtype=jnp.int32)[:, None, None]
    drawn = jax.random.randint(key, (SAMPLES, NLAT, NLON), 0, 9 * NLAT * span)
    keep_level = (NLAT + 2 * latitude) * (span + 2 * sample_index)
    return (drawn >= keep_level).astype(jnp.int32)


def with_ends(array, key, smallest, high):
    longest = array.shape.index(max(array.shape))
    spots = []
    for shift in (0, 1):
        where = [jax.random.randint(jax.random.fold_in(key, axis), (), 0, length) for axis, length in enumerate(array.shape)]
        where[longest] = (where[longest] + shift) % array.shape[longest]
        spots.append(tuple(where))
    return array.at[spots[0]].set(smallest).at[spots[1]].set(high)


def block_levels(key, extent, shards, least, largest):
    def one(dim, blocks):
        heights = jax.random.uniform(jax.random.fold_in(jax.random.fold_in(key, 6), dim), (blocks,), jnp.float32, least / len(shards), largest / len(shards))
        return jnp.repeat(jnp.exp(heights), extent[dim] // blocks).reshape((-1,) + (1,) * (len(extent) - dim - 1))

    gain = one(*shards[0])
    for cut in shards[1:]:
        gain = gain * one(*cut)
    return gain


def normal_values(own_key, extent, deviation, limit, cuts=(), kind=jnp.bfloat16):
    result = jax.random.normal(own_key, extent, jnp.float32) * deviation
    if len(cuts) > 0:
        result = block_levels(own_key, extent, cuts, -0.22, 0.18) * result
    return jnp.clip(result, min=-limit, max=limit).astype(kind)


def setup_inputs(seed: int = 0) -> dict:
    key_of = jax.random.split(jax.random.key(seed), 21)
    return {
        "inputs": normal_values(key_of[0], (SAMPLES, CH, NLAT, NLON), 1.0, 6.0, ((0, 4), (2, 8)), jnp.float32),
        "targets": normal_values(key_of[1], (SAMPLES, CH, NLAT, NLON), 1.0, 6.0, ((0, 4), (2, 8)), jnp.float32),
        "land_mask": with_ends((jax.random.randint(key_of[2], (NLAT, NLON), 0, 10) < 3).astype(jnp.int32), jax.random.fold_in(key_of[2], 1), 0, 1),
        "missing_mask": draw_missing_mask(jax.random.fold_in(key_of[20], 71), 0),
        "order_map": jax.random.permutation(key_of[4], MS).astype(jnp.int32),
        "degree_map": jax.random.permutation(key_of[5], LS).astype(jnp.int32),
        "forward_table": normal_values(key_of[6], (MS, NLAT, LS), NLAT ** -0.5, 1.0, ((0, 8),), jnp.float32),
        "inverse_table": normal_values(key_of[7], (MS, LS, NLAT), L ** -0.5, 0.3125, ((0, 8),), jnp.float32),
        "spectral_weight": normal_values(key_of[8], (LS, 2, C, C), (2 * C) ** -0.5, 0.25, ((0, 8),), jnp.float32),
        "spectral_first": normal_values(key_of[9], (LS, 2, C, C), (0.00011 / NPARAM ** 0.5), 8.940696716308594e-08, ((0, 8),), jnp.float32),
        "spectral_second": jnp.clip(jnp.exp(math.log(8.423440243212067e-17) - 1.3862944 * jax.random.uniform(key_of[10], (LS, 2, C, C), jnp.float32) ** block_levels(key_of[10], (LS, 2, C, C), ((0, 8),), -0.2, 0.2)), 2.105860060803017e-17, 8.423440243212067e-17),
        "io_weight": normal_values(key_of[11], (2, CH, C), ((CH + C) // 2) ** -0.5, 0.5, (), jnp.float32),
        "io_first": normal_values(key_of[12], (2, CH, C), (0.00011 / NPARAM ** 0.5), 8.940696716308594e-08, (), jnp.float32),
        "io_second": jnp.clip(jnp.exp(jax.random.uniform(key_of[13], (2, CH, C), jnp.float32, math.log(2.105860060803017e-17), math.log(8.423440243212067e-17))), 2.105860060803017e-17, 8.423440243212067e-17),
        "mlp_weight": normal_values(key_of[14], (2, C, HID), C ** -0.5, 0.375, (), jnp.float32),
        "mlp_first": normal_values(key_of[15], (2, C, HID), (0.00011 / NPARAM ** 0.5), 8.940696716308594e-08, (), jnp.float32),
        "mlp_second": jnp.clip(jnp.exp(jax.random.uniform(key_of[16], (2, C, HID), jnp.float32, math.log(2.105860060803017e-17), math.log(8.423440243212067e-17))), 2.105860060803017e-17, 8.423440243212067e-17),
        "biases": normal_values(key_of[17], (BIAS,), 0.3, 3.0, (), jnp.float32),
        "bias_first": normal_values(key_of[18], (BIAS,), (0.00033 / NPARAM ** 0.5), 2.980232238769531e-07, (), jnp.float32),
        "bias_second": jnp.clip(jnp.exp(jax.random.uniform(key_of[19], (BIAS,), jnp.float32, math.log(1.8952740712663274e-16), math.log(7.58109628506531e-16))), 1.8952740712663274e-16, 7.58109628506531e-16),
    }


HIGHEST = lax.Precision.HIGHEST
CLIP_LIMIT = 0.001
LEARN_RATE = 0.1
BETA_ONE = 0.9
BETA_TWO = 0.999
EPSILON = 1e-08
WEIGHT_DECAY = 0.1

def smooth(values):
    return jax.nn.gelu(values, approximate=True)

def dft_tables(order_map, lon_count):
    columns = jnp.arange(lon_count, dtype=jnp.int32)
    phase_angle = (order_map[:, None] * columns[None, :] % lon_count).astype(jnp.float32) * (2.0 * math.pi / lon_count)
    cosine = jnp.cos(phase_angle)
    sine_part = jnp.sin(phase_angle)
    forward = jnp.stack([cosine, -sine_part], axis=1) / lon_count
    factor = jnp.where(order_map == 0, 1.0, 2.0).astype(jnp.float32)
    inverse = factor[:, None, None] * jnp.stack([cosine, -sine_part], axis=1)
    return (forward, inverse)

def triangle_mask(orders, degree_map):
    live = (degree_map[None, :] >= orders[:, None]) & (orders[:, None] < M) & (degree_map[None, :] < L)
    return live.astype(jnp.float32)

def complex_block(weight):
    real_part = weight[:, 0]
    imag_part = weight[:, 1]
    top_half = jnp.concatenate([real_part, imag_part], axis=2)
    bottom_half = jnp.concatenate([-imag_part, real_part], axis=2)
    return jnp.concatenate([top_half, bottom_half], axis=1)

def pixel_weights(land_mask, missing_rows, first_row, lat_total, channels):
    lat_dev = land_mask.shape[0]
    latitude = (first_row + jnp.arange(lat_dev, dtype=jnp.int32)).astype(jnp.float32)
    cos_lat = jnp.sin(math.pi * (latitude + 0.5) / lat_total)
    sea_part = (1 - land_mask).astype(jnp.float32)
    valid_part = (1 - missing_rows).astype(jnp.float32) * cos_lat[:, None]
    sea_only = (jnp.arange(channels, dtype=jnp.int32) < SEA_CH)[:, None, None]
    return jnp.where(sea_only, sea_part[None], 1.0) * valid_part[None]

def adam_step(weight, moment_one, moment_two, gradient, decay_rate):
    first_new = BETA_ONE * moment_one + (1.0 - BETA_ONE) * gradient
    second_new = BETA_TWO * moment_two + (1.0 - BETA_TWO) * gradient * gradient
    first_hat = first_new / (1.0 - BETA_ONE ** STEP)
    second_hat = second_new / (1.0 - BETA_TWO ** STEP)
    weight_new = weight - LEARN_RATE * (first_hat / (jnp.sqrt(second_hat) + EPSILON) + decay_rate * weight)
    return (weight_new, first_new, second_new)

def sample_loss(params, fields, truth, pixel_weight, tables):
    spectral_weight, io_weight, mlp_weight, biases = params
    forward, inverse, fwd_masked, inv_masked = tables
    enc_bias = biases[:C]
    hidden_bias = biases[C:C + HID]
    mlp_bias = biases[C + HID:2 * C + HID]
    out_bias = biases[2 * C + HID:]
    encoded = jnp.einsum('caj,ck->ajk', fields, io_weight[0], precision=HIGHEST) + enc_bias
    spectra = jnp.einsum('ajc,spj->aspc', encoded, forward, precision=HIGHEST).reshape(NLAT, MS, 2 * C)
    coeffs = jnp.einsum('sat,ask->tsk', fwd_masked, spectra, precision=HIGHEST)
    mixed_coef = jnp.einsum('tsk,tkj->tsj', coeffs, complex_block(spectral_weight), precision=HIGHEST)
    grid_coef = jnp.einsum('sta,tsk->ask', inv_masked, mixed_coef, precision=HIGHEST).reshape(NLAT, MS, 2, C)
    mixed_in = encoded + jnp.einsum('aspc,spj->ajc', grid_coef, inverse, precision=HIGHEST)
    hidden_pre = jnp.einsum('ajk,kh->ajh', mixed_in, mlp_weight[0], precision=HIGHEST) + hidden_bias
    latent = mixed_in + jnp.einsum('ajh,kh->ajk', smooth(hidden_pre), mlp_weight[1], precision=HIGHEST) + mlp_bias
    predicted = jnp.einsum('ajk,ck->caj', latent, io_weight[1], precision=HIGHEST) + out_bias[:, None, None]
    misfit = predicted - truth
    return jnp.sum(pixel_weight * misfit * misfit)

def reference(inputs, targets, land_mask, missing_mask, order_map, degree_map, forward_table, inverse_table, spectral_weight, spectral_first, spectral_second, io_weight, io_first, io_second, mlp_weight, mlp_first, mlp_second, biases, bias_first, bias_second):
    forward, inverse = dft_tables(order_map, NLON)
    triangle = triangle_mask(order_map, degree_map)
    tables = (forward, inverse, forward_table * triangle[:, None, :], inverse_table * triangle[:, :, None])
    pixel_all = jax.vmap(lambda missing_rows: pixel_weights(land_mask, missing_rows, 0, NLAT, CH))(missing_mask)
    valid_weight = jnp.sum(pixel_all)
    params = (spectral_weight, io_weight, mlp_weight, biases)

    def one_sample(carry, item):
        grads_sum, loss_total = carry
        fields, truth, pixel_weight = item
        loss_value, pull_back = jax.vjp(lambda p: sample_loss(p, fields, truth, pixel_weight, tables), params)
        sample_grads = pull_back(1.0 / valid_weight)[0]
        grads_sum = jax.tree.map(lambda left, right: left + right, grads_sum, sample_grads)
        return ((grads_sum, loss_total + loss_value), None)
    zero_grads = jax.tree.map(jnp.zeros_like, params)
    (grads, loss_sum), _ = lax.scan(one_sample, (zero_grads, jnp.zeros((), jnp.float32)), (inputs, targets, pixel_all))
    squares = jnp.sum(grads[0] * grads[0]) + jnp.sum(grads[1] * grads[1]) + jnp.sum(grads[2] * grads[2]) + jnp.sum(grads[3] * grads[3])
    grad_norm = jnp.sqrt(squares)
    factor = CLIP_LIMIT / jnp.maximum(grad_norm, CLIP_LIMIT)
    states = ((spectral_weight, spectral_first, spectral_second), (io_weight, io_first, io_second), (mlp_weight, mlp_first, mlp_second), (biases, bias_first, bias_second))
    decays = (WEIGHT_DECAY, WEIGHT_DECAY, WEIGHT_DECAY, 0.0)
    results = []
    for index in range(4):
        weight, moment_one, moment_two = states[index]
        weight_new, first_new, second_new = adam_step(weight, moment_one, moment_two, grads[index] * factor, decays[index])
        results += [weight_new, first_new, second_new, weight_new.astype(jnp.bfloat16)]
    return (loss_sum, valid_weight, grad_norm, results[0], results[1], results[2], results[3], results[4], results[5], results[6], results[7], results[8], results[9], results[10], results[11], results[12], results[13], results[14], results[15])
```

```python
import math

import jax
import jax.numpy as jnp
import numpy as np
from jax import lax
from jax.sharding import PartitionSpec as P

M = 360
L = 360
SEA_CH = 1
STEP = 5


HIGH = lax.Precision.HIGH
CLIP_LIMIT = 0.001
LEARN_RATE = 0.1
BETA_ONE = 0.9
BETA_TWO = 0.999
EPSILON = 1e-08
WEIGHT_DECAY = 0.1


def smooth(values):
    return jax.nn.gelu(values, approximate=True)


def dot(spec, left, right):
    return jnp.einsum(spec, left, right, precision=HIGH)


def dft_tables(order_count, lon_count):
    orders = np.arange(order_count, dtype=np.int64)[:, None]
    columns = np.arange(lon_count, dtype=np.int64)[None, :]
    angle = (orders * columns % lon_count) * (2.0 * math.pi / lon_count)
    both = np.stack([np.cos(angle), -np.sin(angle)], axis=1)
    factor = np.where(orders == 0, 1.0, 2.0)[:, :, None]
    return (both / lon_count).astype(np.float32), (factor * both).astype(np.float32)


def pixel_weights(land_mask, missing_rows, first_row, lat_total, channels):
    lat_dev = land_mask.shape[0]
    latitude = (first_row + jnp.arange(lat_dev, dtype=jnp.int32)).astype(jnp.float32)
    cos_lat = jnp.sin(math.pi * (latitude + 0.5) / lat_total)
    sea_part = (1 - land_mask).astype(jnp.float32)
    valid_part = (1 - missing_rows).astype(jnp.float32) * cos_lat[:, None]
    sea_only = (jnp.arange(channels, dtype=jnp.int32) < SEA_CH)[:, None, None]
    return jnp.where(sea_only, sea_part[None], 1.0) * valid_part[None]


def adam_step(weight, moment_one, moment_two, gradient, decay_rate):
    first_new = BETA_ONE * moment_one + (1.0 - BETA_ONE) * gradient
    second_new = BETA_TWO * moment_two + (1.0 - BETA_TWO) * gradient * gradient
    first_hat = first_new / (1.0 - BETA_ONE**STEP)
    second_hat = second_new / (1.0 - BETA_TWO**STEP)
    weight_new = weight - LEARN_RATE * (
        first_hat / (jnp.sqrt(second_hat) + EPSILON) + decay_rate * weight
    )
    return (weight_new, first_new, second_new)


def body(
    inputs,
    targets,
    land_mask,
    missing_mask,
    order_map,
    degree_map,
    forward_table,
    inverse_table,
    spectral_weight,
    spectral_first,
    spectral_second,
    io_weight,
    io_first,
    io_second,
    mlp_weight,
    mlp_first,
    mlp_second,
    biases,
    bias_first,
    bias_second,
):
    fields = inputs[0]
    truth = targets[0]
    lat_dev = fields.shape[1]
    lon_count = fields.shape[2]
    channels = io_weight.shape[1]
    width = io_weight.shape[2]
    hidden_units = mlp_weight.shape[2]
    wide_count = lax.axis_size("wide")
    position = lax.axis_index("wide")
    order_count = order_map.shape[0]
    degree_slots = spectral_weight.shape[0]
    lat_total = lat_dev * wide_count
    entries = lax.axis_size("dp") * channels * lat_total * lon_count
    forward, inverse = dft_tables(order_count, lon_count)

    enc_bias = biases[:width]
    hidden_bias = biases[width : width + hidden_units]
    mlp_bias = biases[width + hidden_units : 2 * width + hidden_units]
    out_bias = biases[2 * width + hidden_units :]
    encoder = jnp.concatenate([io_weight[0], enc_bias[None]], axis=0)

    my_degrees = lax.dynamic_slice_in_dim(degree_map, position * degree_slots, degree_slots)
    slot_of = jnp.argsort(order_map)
    fwd_table = lax.all_to_all(forward_table, "wide", split_axis=2, concat_axis=0, tiled=True)
    inv_table = lax.all_to_all(inverse_table, "wide", split_axis=1, concat_axis=0, tiled=True)
    orders = jnp.arange(order_count, dtype=jnp.int32)
    live = (
        (my_degrees[None, :] >= orders[:, None]) & (orders[:, None] < M) & (my_degrees[None, :] < L)
    ).astype(jnp.float32)
    fwd_masked = fwd_table[slot_of] * live[:, None, :]
    inv_masked = inv_table[slot_of] * live[:, :, None]

    spectra = dot("caj,spj->aspc", fields, forward)
    spectra = lax.all_gather(spectra, "wide", axis=0, tiled=True)
    ones_row = jnp.asarray(forward.astype(np.float64).sum(axis=2).astype(np.float32))
    spectra = jnp.concatenate(
        [spectra, jnp.broadcast_to(ones_row[None, :, :, None], (lat_total, order_count, 2, 1))], axis=3
    )
    coeffs = dot("sat,aspc->tspc", fwd_masked, spectra)
    folded = dot("cd,tpdk->tpck", encoder, spectral_weight)
    out_re = dot("tsc,tck->tsk", coeffs[:, :, 0], folded[:, 0]) - dot(
        "tsc,tck->tsk", coeffs[:, :, 1], folded[:, 1]
    )
    out_im = dot("tsc,tck->tsk", coeffs[:, :, 0], folded[:, 1]) + dot(
        "tsc,tck->tsk", coeffs[:, :, 1], folded[:, 0]
    )
    mixed_coef = jnp.concatenate([out_re, out_im], axis=2)
    grid_coef = dot("sta,tsk->ask", inv_masked, mixed_coef)
    grid_coef = lax.psum_scatter(grid_coef, "wide", scatter_dimension=0, tiled=True)
    grid_coef = grid_coef.reshape(lat_dev, order_count, 2, width)

    encoded = dot("caj,ck->ajk", fields, io_weight[0]) + enc_bias
    mixed_in = encoded + dot("aspc,spj->ajc", grid_coef, inverse)
    hidden_pre = dot("ajk,kh->ajh", mixed_in, mlp_weight[0]) + hidden_bias
    hidden_act, smooth_back = jax.vjp(smooth, hidden_pre)
    latent = mixed_in + dot("ajh,kh->ajk", hidden_act, mlp_weight[1]) + mlp_bias
    predicted = dot("ajk,ck->caj", latent, io_weight[1]) + out_bias[:, None, None]
    misfit = predicted - truth
    pixel_weight = pixel_weights(land_mask, missing_mask[0], position * lat_dev, lat_total, channels)
    count_local = jnp.sum(pixel_weight)
    weighted = pixel_weight * misfit
    loss_local = jnp.sum(weighted * misfit)
    pred_grad = weighted * (2.0 / entries)
    out_bias_grad = jnp.sum(pred_grad, axis=(1, 2))
    decoder_grad = dot("caj,ajk->ck", pred_grad, latent)
    latent_grad = dot("caj,ck->ajk", pred_grad, io_weight[1])
    mlp_bias_grad = jnp.sum(latent_grad, axis=(0, 1))
    down_grad = dot("ajk,ajh->kh", latent_grad, hidden_act)
    act_grad = dot("ajk,kh->ajh", latent_grad, mlp_weight[1])
    pre_grad = smooth_back(act_grad)[0]
    hidden_bias_grad = jnp.sum(pre_grad, axis=(0, 1))
    up_grad = dot("ajk,ajh->kh", mixed_in, pre_grad)
    mixed_grad = latent_grad + dot("ajh,kh->ajk", pre_grad, mlp_weight[0])

    grid_grad = dot("ajc,spj->aspc", mixed_grad, inverse).reshape(lat_dev, order_count, 2 * width)
    grid_grad = lax.all_gather(grid_grad, "wide", axis=0, tiled=True)
    out_grad = dot("sta,ask->tsk", inv_masked, grid_grad)
    out_re_grad, out_im_grad = out_grad[:, :, :width], out_grad[:, :, width:]
    real_part = dot("tsc,tsk->tck", coeffs[:, :, 0], out_re_grad) + dot(
        "tsc,tsk->tck", coeffs[:, :, 1], out_im_grad
    )
    imag_part = dot("tsc,tsk->tck", coeffs[:, :, 0], out_im_grad) - dot(
        "tsc,tsk->tck", coeffs[:, :, 1], out_re_grad
    )
    thin = jnp.stack([real_part, imag_part], axis=1)
    encoder_grad = dot("tpck,tpdk->cd", thin, spectral_weight)
    direct = dot("caj,ajk->ck", fields, mixed_grad)
    direct_bias = jnp.sum(mixed_grad, axis=(0, 1))
    encoder_grad = encoder_grad + jnp.concatenate([direct, direct_bias[None]], axis=0)
    io_grad = jnp.stack([encoder_grad[:channels], decoder_grad])
    mlp_grad = jnp.stack([up_grad, down_grad])
    bias_grad = jnp.concatenate(
        [encoder_grad[channels], hidden_bias_grad, mlp_bias_grad, out_bias_grad]
    )
    io_grad, mlp_grad, bias_grad, loss_sum, valid_weight = lax.psum(
        (io_grad, mlp_grad, bias_grad, loss_local, count_local), ("dp", "wide")
    )
    thin = lax.psum(thin, "dp")
    gram = jnp.einsum("ck,dk->cd", encoder, encoder, precision=lax.Precision.HIGHEST)
    spectral_squares = jnp.sum(thin * jnp.einsum("cd,tpdk->tpck", gram, thin, precision=lax.Precision.HIGHEST))
    spectral_squares = lax.psum(spectral_squares, "wide")
    rescale = entries / valid_weight
    squares = (
        spectral_squares
        + jnp.sum(io_grad * io_grad)
        + jnp.sum(mlp_grad * mlp_grad)
        + jnp.sum(bias_grad * bias_grad)
    )
    grad_norm = jnp.sqrt(squares) * rescale
    factor = rescale * CLIP_LIMIT / jnp.maximum(grad_norm, CLIP_LIMIT)
    spectral_total = dot("cd,tpck->tpdk", encoder, thin)
    spectral_new, spectral_first_new, spectral_second_new = adam_step(
        spectral_weight, spectral_first, spectral_second, spectral_total * factor, WEIGHT_DECAY
    )
    io_new, io_first_new, io_second_new = adam_step(
        io_weight, io_first, io_second, io_grad * factor, WEIGHT_DECAY
    )
    mlp_new, mlp_first_new, mlp_second_new = adam_step(
        mlp_weight, mlp_first, mlp_second, mlp_grad * factor, WEIGHT_DECAY
    )
    bias_new, bias_first_new, bias_second_new = adam_step(
        biases, bias_first, bias_second, bias_grad * factor, 0.0
    )
    return (
        loss_sum,
        valid_weight,
        grad_norm,
        spectral_new,
        spectral_first_new,
        spectral_second_new,
        spectral_new.astype(jnp.bfloat16),
        io_new,
        io_first_new,
        io_second_new,
        io_new.astype(jnp.bfloat16),
        mlp_new,
        mlp_first_new,
        mlp_second_new,
        mlp_new.astype(jnp.bfloat16),
        bias_new,
        bias_first_new,
        bias_second_new,
        bias_new.astype(jnp.bfloat16),
    )


def solution(mesh):
    wide4 = P("wide", None, None, None)
    in_specs = (
        P("dp", None, "wide", None),
        P("dp", None, "wide", None),
        P("wide", None),
        P("dp", "wide", None),
        P(),
        P(),
        P("wide", None, None),
        P("wide", None, None),
        wide4,
        wide4,
        wide4,
    ) + (P(),) * 9
    out_specs = (P(),) * 3 + (wide4,) * 4 + (P(),) * 12
    return jax.shard_map(body, mesh=mesh, in_specs=in_specs, out_specs=out_specs, check_vma=False)
```

```python
import functools
import math

import jax
import jax.numpy as jnp
import numpy as np
from jax import lax
from jax.experimental import pallas as pl
from jax.experimental.pallas import tpu as pltpu
from jax.sharding import PartitionSpec as P

M = 360
L = 360
SEA_CH = 1
STEP = 5


HIGH = lax.Precision.HIGH
CLIP_LIMIT = 0.001
LEARN_RATE = 0.1
BETA_ONE = 0.9
BETA_TWO = 0.999
EPSILON = 1e-08
WEIGHT_DECAY = 0.1


def smooth(values):
    return jax.nn.gelu(values, approximate=True)


def dot(spec, left, right):
    return jnp.einsum(spec, left, right, precision=HIGH)


def dft_tables(order_count, lon_count):
    orders = np.arange(order_count, dtype=np.int64)[:, None]
    columns = np.arange(lon_count, dtype=np.int64)[None, :]
    angle = (orders * columns % lon_count) * (2.0 * math.pi / lon_count)
    both = np.stack([np.cos(angle), -np.sin(angle)], axis=0)
    factor = np.where(orders == 0, 1.0, 2.0)[None]
    return (both / lon_count).astype(np.float32), (factor * both).astype(np.float32)


def halves(value):
    high = value.astype(jnp.bfloat16)
    low = (value - high.astype(jnp.float32)).astype(jnp.bfloat16)
    return high, low


def dot3(left, right, dims=(((1,), (0,)), ((), ()))):
    left_high, left_low = halves(left)
    right_high, right_low = halves(right)

    def one(a, b):
        return lax.dot_general(a, b, dims, preferred_element_type=jnp.float32)

    return one(left_high, right_high) + (one(left_high, right_low) + one(left_low, right_high))


def block_diagonal(rows):
    count, lanes = rows.shape
    spread = jnp.broadcast_to(rows[:, None, :], (count, 8, lanes))
    sub = lax.broadcasted_iota(jnp.int32, (count, 8, lanes), 1)
    lane = lax.broadcasted_iota(jnp.int32, (count, 8, lanes), 2) & 7
    return jnp.where(sub == lane, spread, 0.0).reshape(count * 8, lanes)


def steps(count):
    return max(size for size in range(1, 6) if count % size == 0)


def coefficients(spec_ref, fwd_ref, coef_ref, group):
    rows = pl.ds(pl.multiple_of(group * 8, 8), 8)
    spectra = spec_ref[:, rows, :]
    lat, _, thin = spectra.shape
    product = dot3(block_diagonal(fwd_ref[group]), spectra.reshape(lat * 8, thin))
    coef_ref[:, rows, :] = product.reshape(product.shape[0] // 8, 8, thin)


def forward_kernel(spec_ref, fwd_ref, inv_ref, folded_ref, grid_ref, coef_ref, mixed_ref):
    groups = fwd_ref.shape[0]
    degrees = folded_ref.shape[0]
    slots = mixed_ref.shape[0]
    for spare in range(degrees, slots):
        mixed_ref[spare] = jnp.zeros(mixed_ref.shape[1:], jnp.float32)

    def analyse(group, carry):
        coefficients(spec_ref, fwd_ref, coef_ref, group)
        return carry

    lax.fori_loop(0, groups, analyse, 0, unroll=steps(groups))

    def mix(degree, carry):
        real = folded_ref[degree, 0]
        imag = folded_ref[degree, 1]
        block = jnp.concatenate(
            [jnp.concatenate([real, imag], axis=1), jnp.concatenate([-imag, real], axis=1)], axis=0
        )
        mixed_ref[degree] = dot3(coef_ref[degree], block)
        return carry

    lax.fori_loop(0, degrees, mix, 0, unroll=steps(degrees))

    def synthesise(group, carry):
        rows = pl.ds(pl.multiple_of(group * 8, 8), 8)
        mixed = mixed_ref[:, rows, :]
        product = dot3(
            block_diagonal(inv_ref[group]),
            mixed.reshape(slots * 8, mixed.shape[2]),
            (((0,), (0,)), ((), ())),
        )
        grid_ref[:, rows, :] = product.reshape(product.shape[0] // 8, 8, mixed.shape[2])
        return carry

    lax.fori_loop(0, groups, synthesise, 0, unroll=steps(groups))


def backward_kernel(grid_ref, spec_ref, fwd_ref, inv_ref, thin_ref, coef_ref, out_ref):
    groups = fwd_ref.shape[0]
    degrees, _, channels, width = thin_ref.shape

    @pl.when(pl.program_id(0) == 0)
    def _():
        thin_ref[...] = jnp.zeros(thin_ref.shape, jnp.float32)

    def analyse(group, carry):
        coefficients(spec_ref, fwd_ref, coef_ref, group)
        coefficients(grid_ref, inv_ref, out_ref, group)
        return carry

    lax.fori_loop(0, groups, analyse, 0, unroll=steps(groups))

    def product(degree, carry):
        both = dot3(coef_ref[degree], out_ref[degree], (((0,), (0,)), ((), ())))
        thin_ref[degree, 0] += both[:channels, :width] + both[channels:, width:]
        thin_ref[degree, 1] += both[:channels, width:] - both[channels:, :width]
        return carry

    lax.fori_loop(0, degrees, product, 0, unroll=steps(degrees))


def adam_kernel(
    factor_ref, encoder_ref, thin_ref, weight_ref, first_ref, second_ref,
    weight_out, first_out, second_out, low_out,
):
    factor = factor_ref[0]
    encoder_high, encoder_low = halves(encoder_ref[...])
    left = jnp.concatenate([encoder_high, encoder_high, encoder_low], axis=0)
    for degree, part in np.ndindex(thin_ref.shape[:2]):
        high, low = halves(thin_ref[degree, part] * factor)
        right = jnp.concatenate([high, low, high], axis=0)
        gradient = lax.dot_general(
            left, right, (((0,), (0,)), ((), ())), preferred_element_type=jnp.float32
        )
        weight, first, second = adam_step(
            weight_ref[degree, part], first_ref[degree, part], second_ref[degree, part], gradient, WEIGHT_DECAY
        )
        weight_out[degree, part] = weight
        first_out[degree, part] = first
        second_out[degree, part] = second
        low_out[degree, part] = weight.astype(jnp.bfloat16)


def table_kernel(own, me_ref, slot_ref, wire_ref, degree_ref, place_ref, *rows_refs):
    groups, slots, lanes = rows_refs[0].shape
    lat = lanes // 8
    per_tile = 128 // lat
    degree = degree_ref[...]
    count = degree.shape[0]
    lane = lax.broadcasted_iota(jnp.int32, (count, 128), 1) // lat
    me = me_ref[0]

    def one_group(group, carry):
        found = ([], [])
        for first in range(0, 8, per_tile):
            tiles = [jnp.zeros((count, 128), jnp.float32)] * 2
            for place in range(per_tile):
                order = group * 8 + first + place
                slot = slot_ref[order]
                source = slot // own
                at = slot - source * own
                block = at // per_tile
                columns = pl.ds(pl.multiple_of(block * 128, 128), 128)
                shift = lax.rem((place - (at - block * per_tile)) * lat + 128, 128)
                live = (degree >= order) & (order < M) & (degree < L) & (lane == place)
                for table in range(2):
                    both = [wire_ref[(2 * table + half) ^ me, source, :, columns] for half in range(2)]
                    moved = pltpu.roll(jnp.concatenate(both, axis=0), shift, 1)
                    tiles[table] = jnp.where(live, moved, tiles[table])
            for table in range(2):
                found[table].append(tiles[table])
        place = place_ref[...]
        for table in range(2):
            high, low = halves(jnp.concatenate(found[table], axis=1))
            rows = jnp.dot(high, place, preferred_element_type=jnp.float32)
            rows += jnp.dot(low, place, preferred_element_type=jnp.float32)
            rows_refs[table][group] = rows[:slots]
        return carry

    lax.fori_loop(0, groups, one_group, 0, unroll=steps(groups))


def order_chunk(order_count, lat_total, width):
    best = 8
    for size in range(8, order_count + 1, 8):
        if order_count % size == 0 and lat_total * size * width * 8 <= 8.5 * 2**20:
            best = size
    return best


def vmem(mebibytes):
    return pltpu.CompilerParams(
        dimension_semantics=("arbitrary",), vmem_limit_bytes=mebibytes * 2**20
    )


def table_rows(wire, slot_of, degrees, own, lat_total, slots):
    groups = slot_of.shape[0] // 8
    lane = np.arange(lat_total * 8)
    place = np.zeros((lat_total * 8, lat_total * 8), np.float32)
    place[lane, lane % lat_total * 8 + lane // lat_total] = 1.0
    return pl.pallas_call(
        functools.partial(table_kernel, own),
        in_specs=[pl.BlockSpec(memory_space=pltpu.SMEM)] * 2
        + [pl.BlockSpec(memory_space=pltpu.VMEM)] * 3,
        out_specs=[pl.BlockSpec(memory_space=pltpu.VMEM)] * 2,
        out_shape=[jax.ShapeDtypeStruct((groups, slots, lat_total * 8), jnp.float32)] * 2,
        compiler_params=pltpu.CompilerParams(vmem_limit_bytes=32 * 2**20),
        name="table_rows",
    )(lax.axis_index("dp")[None], slot_of, wire, degrees[:, None], jnp.asarray(place, jnp.bfloat16))


def exchange(value, axis, count, bit):
    return lax.ppermute(value, axis, [(i, i ^ bit) for i in range(count)])


def tables_to_degrees(forward_table, inverse_table, wide_count, degree_slots):
    own, lat_total, order_count = forward_table.shape
    dp_count = lax.axis_size("dp")
    half = -(-degree_slots // 16) * 8
    spare = ((0, 0), (0, 2 * half - degree_slots), (0, -own * lat_total % 128))

    def rows(table):
        table = jnp.pad(table.reshape(wide_count, degree_slots, own * lat_total), spare)
        return table.reshape(wide_count, 2, half, table.shape[2])

    wire = jnp.concatenate(
        [rows(forward_table.transpose(2, 0, 1)), rows(inverse_table.transpose(1, 0, 2))], axis=1
    )
    wire = lax.dynamic_index_in_dim(wire, lax.axis_index("dp"), 1, keepdims=False)
    wire = lax.all_to_all(wire, "wide", split_axis=0, concat_axis=0, tiled=True)
    found = []
    for part, bits in ((wire[: wide_count // 2], (1, 2)), (wire[wide_count // 2 :], (2, 1))):
        by_index = {0: part}
        for bit in bits:
            names = list(by_index)
            passed = exchange(jnp.stack([by_index[i] for i in names]), "dp", dp_count, bit)
            by_index.update({i ^ bit: passed[k] for k, i in enumerate(names)})
        found.append(jnp.stack([by_index[i] for i in range(4)]))
    return jnp.concatenate(found, axis=1)


def all_sum(rows):
    dp_count, wide_count = lax.axis_size("dp"), lax.axis_size("wide")
    if dp_count != 4 or wide_count & (wide_count - 1):
        return lax.psum(rows, ("dp", "wide"))
    me = lax.axis_index("dp")
    piece = rows
    for bit in (1, 2):
        parts = piece.reshape((2, piece.shape[0] // 2) + piece.shape[1:])
        mine = (me & bit) // bit
        sent = lax.dynamic_index_in_dim(parts, 1 - mine, 0, keepdims=False)
        kept = lax.dynamic_index_in_dim(parts, mine, 0, keepdims=False)
        piece = kept + exchange(sent, "dp", dp_count, bit)
    bit = 1
    while bit < wide_count:
        piece = piece + exchange(piece, "wide", wide_count, bit)
        bit *= 2
    for bit in (2, 1):
        other = exchange(piece, "dp", dp_count, bit)
        mine = (me & bit) // bit == 0
        piece = jnp.concatenate(
            [jnp.where(mine, piece, other), jnp.where(mine, other, piece)], axis=0
        )
    return piece


def spectral_forward(spectra, fwd_rows, inv_rows, folded):
    lat_total, order_count, thin = spectra.shape
    degrees, _, channels, width = folded.shape
    slots = fwd_rows.shape[1]
    size = order_chunk(order_count, lat_total, width)
    groups = size // 8
    return pl.pallas_call(
        forward_kernel,
        grid=(order_count // size,),
        in_specs=[
            pl.BlockSpec((lat_total, size, thin), lambda i: (0, i, 0)),
            pl.BlockSpec((groups,) + fwd_rows.shape[1:], lambda i: (i, 0, 0)),
            pl.BlockSpec((groups,) + inv_rows.shape[1:], lambda i: (i, 0, 0)),
            pl.BlockSpec(folded.shape, lambda i: (0, 0, 0, 0)),
        ],
        out_specs=pl.BlockSpec((lat_total, size, 2 * width), lambda i: (0, i, 0)),
        out_shape=jax.ShapeDtypeStruct((lat_total, order_count, 2 * width), jnp.float32),
        scratch_shapes=[
            pltpu.VMEM((slots, size, thin), jnp.float32),
            pltpu.VMEM((slots, size, 2 * width), jnp.float32),
        ],
        compiler_params=vmem(60),
        name="spectral_forward",
    )(spectra, fwd_rows, inv_rows, folded)


def spectral_backward(grid_grad, spectra, fwd_rows, inv_rows, degrees, channels):
    lat_total, order_count, thin = spectra.shape
    width = grid_grad.shape[2] // 2
    slots = fwd_rows.shape[1]
    size = order_chunk(order_count, lat_total, width)
    groups = size // 8
    table = pl.BlockSpec((groups,) + fwd_rows.shape[1:], lambda i: (i, 0, 0))
    return pl.pallas_call(
        backward_kernel,
        grid=(order_count // size,),
        in_specs=[
            pl.BlockSpec((lat_total, size, 2 * width), lambda i: (0, i, 0)),
            pl.BlockSpec((lat_total, size, thin), lambda i: (0, i, 0)),
            table,
            table,
        ],
        out_specs=pl.BlockSpec((degrees, 2, channels, width), lambda i: (0, 0, 0, 0)),
        out_shape=jax.ShapeDtypeStruct((degrees, 2, channels, width), jnp.float32),
        scratch_shapes=[
            pltpu.VMEM((slots, size, thin), jnp.float32),
            pltpu.VMEM((slots, size, 2 * width), jnp.float32),
        ],
        compiler_params=vmem(60),
        name="spectral_backward",
    )(grid_grad, spectra, fwd_rows, inv_rows)


def spectral_adam(factor, encoder, thin, weight, first, second):
    degrees = weight.shape[0]
    size = steps(degrees)
    whole = pl.BlockSpec((size,) + weight.shape[1:], lambda i: (i, 0, 0, 0))
    wide_out = jax.ShapeDtypeStruct(weight.shape, jnp.float32)
    return pl.pallas_call(
        adam_kernel,
        grid=(degrees // size,),
        in_specs=[
            pl.BlockSpec(memory_space=pltpu.SMEM),
            pl.BlockSpec(encoder.shape, lambda i: (0, 0)),
            pl.BlockSpec((size,) + thin.shape[1:], lambda i: (i, 0, 0, 0)),
            whole,
            whole,
            whole,
        ],
        out_specs=[whole] * 4,
        out_shape=[wide_out] * 3 + [jax.ShapeDtypeStruct(weight.shape, jnp.bfloat16)],
        compiler_params=vmem(48),
        name="spectral_adam",
    )(factor, encoder, thin, weight, first, second)


def pixel_weights(land_mask, missing_rows, first_row, lat_total, channels):
    lat_dev = land_mask.shape[0]
    latitude = (first_row + jnp.arange(lat_dev, dtype=jnp.int32)).astype(jnp.float32)
    cos_lat = jnp.sin(math.pi * (latitude + 0.5) / lat_total)
    sea_part = (1 - land_mask).astype(jnp.float32)
    valid_part = (1 - missing_rows).astype(jnp.float32) * cos_lat[:, None]
    sea_only = (jnp.arange(channels, dtype=jnp.int32) < SEA_CH)[:, None, None]
    return jnp.where(sea_only, sea_part[None], 1.0) * valid_part[None]


def adam_step(weight, moment_one, moment_two, gradient, decay_rate):
    first_new = BETA_ONE * moment_one + (1.0 - BETA_ONE) * gradient
    second_new = BETA_TWO * moment_two + (1.0 - BETA_TWO) * gradient * gradient
    first_hat = first_new * (1.0 / (1.0 - BETA_ONE**STEP))
    second_hat = second_new * (1.0 / (1.0 - BETA_TWO**STEP))
    weight_new = weight - LEARN_RATE * (
        first_hat / (jnp.sqrt(second_hat) + EPSILON) + decay_rate * weight
    )
    return (weight_new, first_new, second_new)


def body(
    inputs,
    targets,
    land_mask,
    missing_mask,
    order_map,
    degree_map,
    forward_table,
    inverse_table,
    spectral_weight,
    spectral_first,
    spectral_second,
    io_weight,
    io_first,
    io_second,
    mlp_weight,
    mlp_first,
    mlp_second,
    biases,
    bias_first,
    bias_second,
):
    fields = inputs[0]
    truth = targets[0]
    lat_dev = fields.shape[1]
    lon_count = fields.shape[2]
    channels = io_weight.shape[1]
    width = io_weight.shape[2]
    hidden_units = mlp_weight.shape[2]
    wide_count = lax.axis_size("wide")
    position = lax.axis_index("wide")
    order_count = order_map.shape[0]
    degree_slots = spectral_weight.shape[0]
    lat_total = lat_dev * wide_count
    entries = lax.axis_size("dp") * channels * lat_total * lon_count
    forward, inverse = dft_tables(order_count, lon_count)

    enc_bias = biases[:width]
    hidden_bias = biases[width : width + hidden_units]
    mlp_bias = biases[width + hidden_units : 2 * width + hidden_units]
    out_bias = biases[2 * width + hidden_units :]
    thin_count = -(-(channels + 1) // 16) * 16
    spare = thin_count - channels - 1
    encoder = jnp.concatenate(
        [io_weight[0], enc_bias[None], jnp.zeros((spare, width), jnp.float32)], axis=0
    )

    spectra = dot("caj,psj->pacs", fields, forward)
    spectra = lax.all_gather(spectra, "wide", axis=0, tiled=False)
    ones_row = forward.astype(np.float64).sum(axis=2).astype(np.float32)
    spectra = jnp.concatenate(
        [
            spectra,
            jnp.broadcast_to(ones_row[None, :, None, None, :], (wide_count, 2, lat_dev, 1, order_count)),
            jnp.zeros((wide_count, 2, lat_dev, spare, order_count), jnp.float32),
        ],
        axis=3,
    )
    spectra = spectra.transpose(0, 2, 4, 1, 3).reshape(lat_total, order_count, 2 * thin_count)

    my_degrees = lax.dynamic_slice_in_dim(degree_map, position * degree_slots, degree_slots)
    slot_of = jnp.argsort(order_map)
    slots = degree_slots + degree_slots % 2
    if 128 % lat_total == 0 and lax.axis_size("dp") == 4 and wide_count % 2 == 0:
        wire = tables_to_degrees(forward_table, inverse_table, wide_count, degree_slots)
        degrees = jnp.pad(my_degrees, (0, 2 * wire.shape[2] - degree_slots), constant_values=-1)
        own = forward_table.shape[0]
        fwd_rows, inv_rows = table_rows(wire, slot_of, degrees, own, lat_total, slots)
    else:
        fwd_table = lax.all_to_all(forward_table, "wide", split_axis=2, concat_axis=0, tiled=True)
        inv_table = lax.all_to_all(inverse_table, "wide", split_axis=1, concat_axis=0, tiled=True)
        orders = jnp.arange(order_count, dtype=jnp.int32)
        live = (
            (my_degrees[None, :] >= orders[:, None])
            & (orders[:, None] < M)
            & (my_degrees[None, :] < L)
        ).astype(jnp.float32)
        even = ((0, 0), (0, degree_slots % 2), (0, 0), (0, 0))
        fwd_masked = fwd_table[slot_of] * live[:, None, :]
        inv_masked = inv_table[slot_of] * live[:, :, None]
        fwd_masked = fwd_masked.reshape(order_count // 8, 8, lat_total, degree_slots)
        inv_masked = inv_masked.reshape(order_count // 8, 8, degree_slots, lat_total)

        def by_degree(table):
            return jnp.pad(table, even).reshape(order_count // 8, slots, lat_total * 8)

        fwd_rows = by_degree(fwd_masked.transpose(0, 3, 2, 1))
        inv_rows = by_degree(inv_masked.transpose(0, 2, 3, 1))

    folded = dot("cd,tpdk->tpck", encoder, spectral_weight)
    grid_coef = spectral_forward(spectra, fwd_rows, inv_rows, folded)
    grid_coef = lax.psum_scatter(grid_coef, "wide", scatter_dimension=0, tiled=True)
    grid_coef = grid_coef.reshape(lat_dev, order_count, 2, width)

    encoded = dot("caj,ck->ajk", fields, io_weight[0]) + enc_bias
    mixed_in = encoded + dot("aspc,psj->ajc", grid_coef, inverse)
    hidden_pre = dot("ajk,kh->ajh", mixed_in, mlp_weight[0]) + hidden_bias
    hidden_act, smooth_back = jax.vjp(smooth, hidden_pre)
    latent = mixed_in + dot("ajh,kh->ajk", hidden_act, mlp_weight[1]) + mlp_bias
    predicted = dot("ajk,ck->caj", latent, io_weight[1]) + out_bias[:, None, None]
    misfit = predicted - truth
    pixel_weight = pixel_weights(land_mask, missing_mask[0], position * lat_dev, lat_total, channels)
    count_local = jnp.sum(pixel_weight)
    weighted = pixel_weight * misfit
    loss_local = jnp.sum(weighted * misfit)
    pred_grad = weighted * (2.0 / entries)
    out_bias_grad = jnp.sum(pred_grad, axis=(1, 2))
    decoder_grad = dot("caj,ajk->ck", pred_grad, latent)
    latent_grad = dot("caj,ck->ajk", pred_grad, io_weight[1])
    mlp_bias_grad = jnp.sum(latent_grad, axis=(0, 1))
    down_grad = dot("ajk,ajh->kh", latent_grad, hidden_act)
    act_grad = dot("ajk,kh->ajh", latent_grad, mlp_weight[1])
    pre_grad = smooth_back(act_grad)[0]
    hidden_bias_grad = jnp.sum(pre_grad, axis=(0, 1))
    up_grad = dot("ajk,ajh->kh", mixed_in, pre_grad)
    mixed_grad = latent_grad + dot("ajh,kh->ajk", pre_grad, mlp_weight[0])

    grid_grad = dot("ajc,psj->aspc", mixed_grad, inverse).reshape(lat_dev, order_count, 2 * width)
    grid_grad = lax.all_gather(grid_grad, "wide", axis=0, tiled=True)
    direct = dot("caj,ajk->ck", fields, mixed_grad)
    direct_bias = jnp.sum(mixed_grad, axis=(0, 1))
    small = [direct_bias, hidden_bias_grad, mlp_bias_grad, out_bias_grad, loss_local[None], count_local[None]]
    small = jnp.concatenate(small)
    small_count = small.shape[0]
    flat = [up_grad.reshape(-1, width), down_grad.reshape(-1, width), decoder_grad, direct]
    flat.append(jnp.pad(small, (0, -small_count % width)).reshape(-1, width))
    flat = jnp.concatenate(flat, axis=0)
    flat = all_sum(jnp.pad(flat, ((0, -flat.shape[0] % 32), (0, 0))))
    grid_grad, flat = lax.optimization_barrier((grid_grad, flat))
    thin = spectral_backward(grid_grad, spectra, fwd_rows, inv_rows, degree_slots, thin_count)
    at = 2 * hidden_units
    mlp_grad = flat[:at].reshape(2, width, hidden_units)
    decoder_grad = flat[at : at + channels]
    direct = flat[at + channels : at + 2 * channels]
    small = flat[at + 2 * channels :].reshape(-1)[:small_count]
    encoder_grad = all_sum(dot("tpck,tpdk->cd", thin, spectral_weight))
    thin = lax.psum(thin, "dp")
    gram = jnp.einsum("ck,dk->cd", encoder, encoder, precision=lax.Precision.HIGHEST)
    spectral_squares = jnp.sum(
        thin * jnp.einsum("cd,tpdk->tpck", gram, thin, precision=lax.Precision.HIGHEST)
    )
    spectral_squares = lax.psum(spectral_squares, "wide")
    io_grad = jnp.stack([direct + encoder_grad[:channels], decoder_grad])
    bias_grad = jnp.concatenate([small[:width] + encoder_grad[channels], small[width:-2]])
    loss_sum, valid_weight = small[-2], small[-1]
    rescale = entries / valid_weight
    squares = (
        spectral_squares
        + jnp.sum(io_grad * io_grad)
        + jnp.sum(mlp_grad * mlp_grad)
        + jnp.sum(bias_grad * bias_grad)
    )
    grad_norm = jnp.sqrt(squares) * rescale
    factor = rescale * CLIP_LIMIT / jnp.maximum(grad_norm, CLIP_LIMIT)
    spectral_new, spectral_first_new, spectral_second_new, spectral_low = spectral_adam(
        factor[None], encoder, thin, spectral_weight, spectral_first, spectral_second
    )
    io_new, io_first_new, io_second_new = adam_step(
        io_weight, io_first, io_second, io_grad * factor, WEIGHT_DECAY
    )
    mlp_new, mlp_first_new, mlp_second_new = adam_step(
        mlp_weight, mlp_first, mlp_second, mlp_grad * factor, WEIGHT_DECAY
    )
    bias_new, bias_first_new, bias_second_new = adam_step(
        biases, bias_first, bias_second, bias_grad * factor, 0.0
    )
    return (
        loss_sum,
        valid_weight,
        grad_norm,
        spectral_new,
        spectral_first_new,
        spectral_second_new,
        spectral_low,
        io_new,
        io_first_new,
        io_second_new,
        io_new.astype(jnp.bfloat16),
        mlp_new,
        mlp_first_new,
        mlp_second_new,
        mlp_new.astype(jnp.bfloat16),
        bias_new,
        bias_first_new,
        bias_second_new,
        bias_new.astype(jnp.bfloat16),
    )


def solution(mesh):
    wide4 = P("wide", None, None, None)
    in_specs = (
        P("dp", None, "wide", None),
        P("dp", None, "wide", None),
        P("wide", None),
        P("dp", "wide", None),
        P(),
        P(),
        P("wide", None, None),
        P("wide", None, None),
        wide4,
        wide4,
        wide4,
    ) + (P(),) * 9
    out_specs = (P(),) * 3 + (wide4,) * 4 + (P(),) * 12
    return jax.shard_map(body, mesh=mesh, in_specs=in_specs, out_specs=out_specs, check_vma=False)
```

```python
import functools
import math

import jax
import jax.numpy as jnp
import numpy as np
from jax import lax
from jax.experimental import pallas as pl
from jax.experimental.pallas import tpu as pltpu
from jax.sharding import PartitionSpec as P

M = 360
L = 360
SEA_CH = 1
STEP = 5


HIGH = lax.Precision.HIGH
CLIP_LIMIT = 0.001
LEARN_RATE = 0.1
BETA_ONE = 0.9
BETA_TWO = 0.999
EPSILON = 1e-08
WEIGHT_DECAY = 0.1


def smooth(values):
    return jax.nn.gelu(values, approximate=True)


def dot(spec, left, right):
    return jnp.einsum(spec, left, right, precision=HIGH)


def dft_tables(order_count, lon_count):
    orders = np.arange(order_count, dtype=np.int64)[:, None]
    columns = np.arange(lon_count, dtype=np.int64)[None, :]
    angle = (orders * columns % lon_count) * (2.0 * math.pi / lon_count)
    both = np.stack([np.cos(angle), -np.sin(angle)], axis=0)
    factor = np.where(orders == 0, 1.0, 2.0)[None]
    return (both / lon_count).astype(np.float32), (factor * both).astype(np.float32)


def halves(value):
    high = value.astype(jnp.bfloat16)
    low = (value - high.astype(jnp.float32)).astype(jnp.bfloat16)
    return high, low


def dot3(left, right, dims=(((1,), (0,)), ((), ()))):
    left_high, left_low = halves(left)
    right_high, right_low = halves(right)

    def one(a, b):
        return lax.dot_general(a, b, dims, preferred_element_type=jnp.float32)

    return one(left_high, right_high) + (one(left_high, right_low) + one(left_low, right_high))


def block_diagonal(rows):
    count, lanes = rows.shape
    spread = jnp.broadcast_to(rows[:, None, :], (count, 8, lanes))
    sub = lax.broadcasted_iota(jnp.int32, (count, 8, lanes), 1)
    lane = lax.broadcasted_iota(jnp.int32, (count, 8, lanes), 2) & 7
    return jnp.where(sub == lane, spread, 0.0).reshape(count * 8, lanes)


def steps(count):
    return max(size for size in range(1, 6) if count % size == 0)


def group_rows(group):
    return pl.ds(pl.multiple_of(group * 8, 8), 8)


def legendre(values, table, out_ref, group):
    lat, _, lanes = values.shape
    product = dot3(block_diagonal(table), values.reshape(lat * 8, lanes))
    out_ref[:, group_rows(group), :] = product.reshape(product.shape[0] // 8, 8, lanes)


def channel_spectra(spec_ref, lat_dev, channels, thin, group):
    devices, _, size, lanes = spec_ref.shape
    real = spec_ref[:, 0, group_rows(group), :].reshape(devices * 8, lanes)
    imag = spec_ref[:, 1, group_rows(group), :].reshape(devices * 8, lanes)
    lane = lax.broadcasted_iota(jnp.int32, (devices * 8, lanes), 1)
    order = lax.broadcasted_iota(jnp.int32, (devices * 8, lanes), 0) & 7
    order += pl.program_id(0) * size + group * 8
    ones = jnp.where((order == 0) & (lane == channels), 1.0, 0.0)
    half = thin // 2
    rows = []
    for row in range(lat_dev):
        base = row * channels
        left = pltpu.roll(real, (lanes - base) % lanes, 1) if base else real
        right = pltpu.roll(imag, (half - base) % lanes, 1)
        value = jnp.where((lane >= half) & (lane < half + channels), right, ones)
        value = jnp.where(lane < channels, left, value)
        rows.append(value[:, :thin].reshape(devices, 8, thin))
    return jnp.stack(rows, axis=1).reshape(devices * lat_dev, 8, thin)


def forward_kernel(lat_dev, channels, spec_ref, fwd_ref, inv_ref, folded_ref, grid_ref, coef_ref, mixed_ref):
    groups = fwd_ref.shape[0]
    degrees = folded_ref.shape[0]
    slots = mixed_ref.shape[0]
    for spare in range(degrees, slots):
        mixed_ref[spare] = jnp.zeros(mixed_ref.shape[1:], jnp.float32)

    thin = coef_ref.shape[2]

    def analyse(group, carry):
        spectra = channel_spectra(spec_ref, lat_dev, channels, thin, group)
        legendre(spectra, fwd_ref[group], coef_ref, group)
        return carry

    lax.fori_loop(0, groups, analyse, 0, unroll=steps(groups))

    def mix(degree, carry):
        real = folded_ref[degree, 0]
        imag = folded_ref[degree, 1]
        block = jnp.concatenate(
            [jnp.concatenate([real, imag], axis=1), jnp.concatenate([-imag, real], axis=1)], axis=0
        )
        mixed_ref[degree] = dot3(coef_ref[degree], block)
        return carry

    lax.fori_loop(0, degrees, mix, 0, unroll=steps(degrees))

    def synthesise(group, carry):
        rows = pl.ds(pl.multiple_of(group * 8, 8), 8)
        mixed = mixed_ref[:, rows, :]
        product = dot3(
            block_diagonal(inv_ref[group]),
            mixed.reshape(slots * 8, mixed.shape[2]),
            (((0,), (0,)), ((), ())),
        )
        grid_ref[:, rows, :] = product.reshape(product.shape[0] // 8, 8, mixed.shape[2])
        return carry

    lax.fori_loop(0, groups, synthesise, 0, unroll=steps(groups))


def backward_kernel(degrees, lat_dev, fields, grid_ref, spec_ref, fwd_ref, inv_ref, thin_ref, coef_ref, out_ref):
    groups = fwd_ref.shape[0]
    _, _, channels, width = thin_ref.shape

    @pl.when(pl.program_id(0) == 0)
    def _():
        thin_ref[...] = jnp.zeros(thin_ref.shape, jnp.float32)

    def analyse(group, carry):
        spectra = channel_spectra(spec_ref, lat_dev, fields, 2 * channels, group)
        legendre(spectra, fwd_ref[group], coef_ref, group)
        legendre(grid_ref[:, group_rows(group), :], inv_ref[group], out_ref, group)
        return carry

    lax.fori_loop(0, groups, analyse, 0, unroll=steps(groups))

    def product(degree, carry):
        both = dot3(coef_ref[degree], out_ref[degree], (((0,), (0,)), ((), ())))
        thin_ref[degree, 0] += both[:channels, :width] + both[channels:, width:]
        thin_ref[degree, 1] += both[:channels, width:] - both[channels:, :width]
        return carry

    lax.fori_loop(0, degrees, product, 0, unroll=steps(degrees))


def adam_kernel(
    factor_ref, encoder_ref, thin_ref, weight_ref, first_ref, second_ref,
    weight_out, first_out, second_out, low_out,
):
    factor = factor_ref[0]
    encoder_high, encoder_low = halves(encoder_ref[...])
    left = jnp.concatenate([encoder_high, encoder_high, encoder_low], axis=0)
    for degree, part in np.ndindex(thin_ref.shape[:2]):
        high, low = halves(thin_ref[degree, part] * factor)
        right = jnp.concatenate([high, low, high], axis=0)
        gradient = lax.dot_general(
            left, right, (((0,), (0,)), ((), ())), preferred_element_type=jnp.float32
        )
        weight, first, second = adam_step(
            weight_ref[degree, part], first_ref[degree, part], second_ref[degree, part], gradient, WEIGHT_DECAY
        )
        weight_out[degree, part] = weight
        first_out[degree, part] = first
        second_out[degree, part] = second
        low_out[degree, part] = weight.astype(jnp.bfloat16)


def table_kernel(own, me_ref, slot_ref, wire_ref, degree_ref, place_ref, *rows_refs):
    groups, slots, lanes = rows_refs[0].shape
    lat = lanes // 8
    per_tile = 128 // lat
    degree = degree_ref[...]
    count = degree.shape[0]
    lane = lax.broadcasted_iota(jnp.int32, (count, 128), 1) // lat
    me = me_ref[0]
    me_wide = me_ref[1]

    def one_group(group, carry):
        found = ([], [])
        for first in range(0, 8, per_tile):
            tiles = [jnp.zeros((count, 128), jnp.float32)] * 2
            for place in range(per_tile):
                order = group * 8 + first + place
                slot = slot_ref[order]
                source = slot // own
                at = slot - source * own
                block = at // per_tile
                columns = pl.ds(pl.multiple_of(block * 128, 128), 128)
                shift = lax.rem((place - (at - block * per_tile)) * lat + 128, 128)
                live = (degree >= order) & (order < M) & (degree < L) & (lane == place)
                for table in range(2):
                    both = [wire_ref[(2 * table + half) ^ me, source ^ me_wide, :, columns] for half in range(2)]
                    moved = pltpu.roll(jnp.concatenate(both, axis=0), shift, 1)
                    tiles[table] = jnp.where(live, moved, tiles[table])
            for table in range(2):
                found[table].append(tiles[table])
        place = place_ref[...]
        for table in range(2):
            high, low = halves(jnp.concatenate(found[table], axis=1))
            rows = jnp.dot(high, place, preferred_element_type=jnp.float32)
            rows += jnp.dot(low, place, preferred_element_type=jnp.float32)
            rows_refs[table][group] = rows[:slots]
        return carry

    lax.fori_loop(0, groups, one_group, 0, unroll=steps(groups))


def order_chunk(order_count, lat_total, width):
    best = 8
    for size in range(8, order_count + 1, 8):
        if order_count % size == 0 and lat_total * size * width * 8 <= 8.5 * 2**20:
            best = size
    return best


def vmem(mebibytes):
    return pltpu.CompilerParams(
        dimension_semantics=("arbitrary",), vmem_limit_bytes=mebibytes * 2**20
    )


def table_rows(wire, slot_of, degrees, own, lat_total, slots):
    groups = slot_of.shape[0] // 8
    lane = np.arange(lat_total * 8)
    place = np.zeros((lat_total * 8, lat_total * 8), np.float32)
    place[lane, lane % lat_total * 8 + lane // lat_total] = 1.0
    return pl.pallas_call(
        functools.partial(table_kernel, own),
        in_specs=[pl.BlockSpec(memory_space=pltpu.SMEM)] * 2
        + [pl.BlockSpec(memory_space=pltpu.VMEM)] * 3,
        out_specs=[pl.BlockSpec(memory_space=pltpu.VMEM)] * 2,
        out_shape=[jax.ShapeDtypeStruct((groups, slots, lat_total * 8), jnp.float32)] * 2,
        compiler_params=pltpu.CompilerParams(vmem_limit_bytes=32 * 2**20),
        name="table_rows",
    )(jnp.stack([lax.axis_index("dp"), lax.axis_index("wide")]), slot_of, wire, degrees[:, None], jnp.asarray(place, jnp.bfloat16))


def exchange(value, axis, count, bit):
    return lax.ppermute(value, axis, [(i, i ^ bit) for i in range(count)])


def wire_kernel(degrees, me_ref, forward_ref, inverse_ref, wire_ref, turned_ref):
    own, lat, order_count = forward_ref.shape
    owners, half, lanes = wire_ref.shape
    per_tile = 128 // lat
    me = me_ref[0]

    @pl.when(me < 2)
    def _():
        turned_ref[order_count:] = jnp.zeros((turned_ref.shape[0] - order_count, lanes), jnp.float32)
        turned_ref[:order_count, : own * lat] = forward_ref[...].reshape(own * lat, order_count).T
        if lanes > own * lat:
            turned_ref[:order_count, own * lat :] = jnp.zeros(
                (order_count, lanes - own * lat), jnp.float32
            )

    def forward_part(part):
        for owner in range(owners):
            first = owner * degrees + part * half
            wire_ref[owner] = turned_ref[first : first + half, :]

    def inverse_part(part):
        lane = lax.broadcasted_iota(jnp.int32, (half, 128), 1) // lat
        for owner in range(owners):
            first = owner * degrees + part * half
            rows = min(half, order_count - first)
            for tile in range(lanes // 128):
                value = jnp.zeros((rows, 128), jnp.float32)
                for place in range(per_tile):
                    slot = tile * per_tile + place
                    if slot < own:
                        found = inverse_ref[slot, first : first + rows, :]
                        found = jnp.concatenate([found] * per_tile, axis=1)
                        value = jnp.where(lane[:rows] == place, found, value)
                columns = slice(tile * 128, tile * 128 + 128)
                wire_ref[owner, :rows, columns] = value
                if rows < half:
                    wire_ref[owner, rows:, columns] = jnp.zeros((half - rows, 128), jnp.float32)

    pl.when(me == 0)(functools.partial(forward_part, 0))
    pl.when(me == 1)(functools.partial(forward_part, 1))
    pl.when(me == 2)(functools.partial(inverse_part, 0))
    pl.when(me == 3)(functools.partial(inverse_part, 1))


def tables_to_degrees(forward_table, inverse_table, wide_count, degree_slots, beside):
    own, lat_total, order_count = forward_table.shape
    dp_count = lax.axis_size("dp")
    half = -(-degree_slots // 16) * 8
    lanes = -(-own * lat_total // 128) * 128
    wire = pl.pallas_call(
        functools.partial(wire_kernel, degree_slots),
        in_specs=[pl.BlockSpec(memory_space=pltpu.SMEM)]
        + [pl.BlockSpec(memory_space=pltpu.VMEM)] * 2,
        out_specs=pl.BlockSpec(memory_space=pltpu.VMEM),
        out_shape=jax.ShapeDtypeStruct((wide_count, half, lanes), jnp.float32),
        scratch_shapes=[pltpu.VMEM((order_count + 2 * half - degree_slots + 8, lanes), jnp.float32)],
        compiler_params=pltpu.CompilerParams(vmem_limit_bytes=32 * 2**20),
        name="table_wire",
    )(lax.axis_index("dp")[None], forward_table, inverse_table)
    me = lax.axis_index("wide")
    pieces = [lax.dynamic_index_in_dim(wire, me ^ k, 0, keepdims=False) for k in range(wide_count)]
    pieces = [pieces[0]] + [exchange(pieces[k], "wide", wide_count, k) for k in range(1, wide_count)]
    wire, beside = lax.optimization_barrier((jnp.stack(pieces), beside))
    found = []
    for part, bits in ((wire[: wide_count // 2], (1, 2)), (wire[wide_count // 2 :], (2, 1))):
        by_index = {0: part}
        for bit in bits:
            names = list(by_index)
            passed = exchange(jnp.stack([by_index[i] for i in names]), "dp", dp_count, bit)
            by_index.update({i ^ bit: passed[k] for k, i in enumerate(names)})
        found.append(jnp.stack([by_index[i] for i in range(4)]))
    return jnp.concatenate(found, axis=1), beside


def reduce_halves(piece, bits):
    me = lax.axis_index("dp")
    for bit in bits:
        parts = piece.reshape((2, piece.shape[0] // 2) + piece.shape[1:])
        mine = (me & bit) // bit
        sent = lax.dynamic_index_in_dim(parts, 1 - mine, 0, keepdims=False)
        kept = lax.dynamic_index_in_dim(parts, mine, 0, keepdims=False)
        piece = kept + exchange(sent, "dp", 4, bit)
    return piece


def gather_halves(piece, bits):
    me = lax.axis_index("dp")
    for bit in bits[::-1]:
        other = exchange(piece, "dp", 4, bit)
        low = me & bit == 0
        piece = jnp.concatenate([jnp.where(low, piece, other), jnp.where(low, other, piece)], axis=0)
    return piece


def wide_sum(piece):
    wide_count = lax.axis_size("wide")
    bit = 1
    while bit < wide_count:
        piece = piece + exchange(piece, "wide", wide_count, bit)
        bit *= 2
    return piece


def by_bits():
    wide_count = lax.axis_size("wide")
    return lax.axis_size("dp") == 4 and wide_count & (wide_count - 1) == 0


def all_sum(rows):
    if not by_bits():
        return lax.psum(rows, ("dp", "wide"))
    return gather_halves(wide_sum(reduce_halves(rows, (1, 2))), (1, 2))


def thin_sum(thin, gram):
    def squares(piece):
        product = jnp.einsum("cd,tdk->tck", gram, piece, precision=lax.Precision.HIGHEST)
        return jnp.sum(piece * product)

    pairs = thin.shape[0]
    if not by_bits() or pairs % 4:
        thin = lax.psum(thin, "dp")
        return thin, lax.psum(squares(thin), "wide")
    cut = pairs // 8 * 4
    halved = [(reduce_halves(thin[:cut], (1, 2)), (1, 2)), (reduce_halves(thin[cut:], (2, 1)), (2, 1))]
    total = jnp.broadcast_to(sum(squares(piece) for piece, _ in halved), (8, 128))
    for bit in (1, 2):
        total = total + exchange(total, "dp", 4, bit)
    total = wide_sum(total)[0, 0]
    return jnp.concatenate([gather_halves(piece, bits) for piece, bits in halved]), total


def spectral_forward(spectra, fwd_rows, inv_rows, folded, lat_dev, fields):
    devices, _, order_count, lanes = spectra.shape
    lat_total = devices * lat_dev
    degrees, _, channels, width = folded.shape
    thin = 2 * channels
    slots = fwd_rows.shape[1]
    size = order_chunk(order_count, lat_total, width)
    groups = size // 8
    return pl.pallas_call(
        functools.partial(forward_kernel, lat_dev, fields),
        grid=(order_count // size,),
        in_specs=[
            pl.BlockSpec((devices, 2, size, lanes), lambda i: (0, 0, i, 0)),
            pl.BlockSpec((groups,) + fwd_rows.shape[1:], lambda i: (i, 0, 0)),
            pl.BlockSpec((groups,) + inv_rows.shape[1:], lambda i: (i, 0, 0)),
            pl.BlockSpec(folded.shape, lambda i: (0, 0, 0, 0)),
        ],
        out_specs=pl.BlockSpec((lat_total, size, 2 * width), lambda i: (0, i, 0)),
        out_shape=jax.ShapeDtypeStruct((lat_total, order_count, 2 * width), jnp.float32),
        scratch_shapes=[
            pltpu.VMEM((slots, size, thin), jnp.float32),
            pltpu.VMEM((slots, size, 2 * width), jnp.float32),
        ],
        compiler_params=vmem(60),
        name="spectral_forward",
    )(spectra, fwd_rows, inv_rows, folded)


def spectral_backward(grid_grad, spectra, fwd_rows, inv_rows, degrees, channels, fields):
    devices, _, order_count, lanes = spectra.shape
    lat_total = grid_grad.shape[0]
    lat_dev = lat_total // devices
    thin = 2 * channels
    width = grid_grad.shape[2] // 2
    slots = fwd_rows.shape[1]
    size = order_chunk(order_count, lat_total, width)
    groups = size // 8
    table = pl.BlockSpec((groups,) + fwd_rows.shape[1:], lambda i: (i, 0, 0))
    return pl.pallas_call(
        functools.partial(backward_kernel, degrees, lat_dev, fields),
        grid=(order_count // size,),
        in_specs=[
            pl.BlockSpec((lat_total, size, 2 * width), lambda i: (0, i, 0)),
            pl.BlockSpec((devices, 2, size, lanes), lambda i: (0, 0, i, 0)),
            table,
            table,
        ],
        out_specs=pl.BlockSpec((slots, 2, channels, width), lambda i: (0, 0, 0, 0)),
        out_shape=jax.ShapeDtypeStruct((slots, 2, channels, width), jnp.float32),
        scratch_shapes=[
            pltpu.VMEM((slots, size, thin), jnp.float32),
            pltpu.VMEM((slots, size, 2 * width), jnp.float32),
        ],
        compiler_params=vmem(60),
        name="spectral_backward",
    )(grid_grad, spectra, fwd_rows, inv_rows)


def spectral_adam(factor, encoder, thin, weight, first, second):
    degrees = weight.shape[0]
    size = steps(degrees)
    whole = pl.BlockSpec((size,) + weight.shape[1:], lambda i: (i, 0, 0, 0))
    wide_out = jax.ShapeDtypeStruct(weight.shape, jnp.float32)
    return pl.pallas_call(
        adam_kernel,
        grid=(degrees // size,),
        in_specs=[
            pl.BlockSpec(memory_space=pltpu.SMEM),
            pl.BlockSpec(encoder.shape, lambda i: (0, 0)),
            pl.BlockSpec((size,) + thin.shape[1:], lambda i: (i, 0, 0, 0)),
            whole,
            whole,
            whole,
        ],
        out_specs=[whole] * 4,
        out_shape=[wide_out] * 3 + [jax.ShapeDtypeStruct(weight.shape, jnp.bfloat16)],
        compiler_params=vmem(48),
        name="spectral_adam",
    )(factor, encoder, thin, weight, first, second)


def pixel_weights(land_mask, missing_rows, first_row, lat_total, channels):
    lat_dev = land_mask.shape[0]
    latitude = (first_row + jnp.arange(lat_dev, dtype=jnp.int32)).astype(jnp.float32)
    cos_lat = jnp.sin(math.pi * (latitude + 0.5) / lat_total)
    sea_part = (1 - land_mask).astype(jnp.float32)
    valid_part = (1 - missing_rows).astype(jnp.float32) * cos_lat[:, None]
    sea_only = (jnp.arange(channels, dtype=jnp.int32) < SEA_CH)[:, None, None]
    return jnp.where(sea_only, sea_part[None], 1.0) * valid_part[None]


def adam_step(weight, moment_one, moment_two, gradient, decay_rate):
    first_new = BETA_ONE * moment_one + (1.0 - BETA_ONE) * gradient
    second_new = BETA_TWO * moment_two + (1.0 - BETA_TWO) * gradient * gradient
    first_hat = first_new * (1.0 / (1.0 - BETA_ONE**STEP))
    second_hat = second_new * (1.0 / (1.0 - BETA_TWO**STEP))
    weight_new = weight - LEARN_RATE * (
        first_hat / (jnp.sqrt(second_hat) + EPSILON) + decay_rate * weight
    )
    return (weight_new, first_new, second_new)


def body(
    inputs,
    targets,
    land_mask,
    missing_mask,
    order_map,
    degree_map,
    forward_table,
    inverse_table,
    spectral_weight,
    spectral_first,
    spectral_second,
    io_weight,
    io_first,
    io_second,
    mlp_weight,
    mlp_first,
    mlp_second,
    biases,
    bias_first,
    bias_second,
):
    fields = inputs[0]
    truth = targets[0]
    lat_dev = fields.shape[1]
    lon_count = fields.shape[2]
    channels = io_weight.shape[1]
    width = io_weight.shape[2]
    hidden_units = mlp_weight.shape[2]
    wide_count = lax.axis_size("wide")
    position = lax.axis_index("wide")
    order_count = order_map.shape[0]
    degree_slots = spectral_weight.shape[0]
    lat_total = lat_dev * wide_count
    entries = lax.axis_size("dp") * channels * lat_total * lon_count
    forward, inverse = dft_tables(order_count, lon_count)

    enc_bias = biases[:width]
    hidden_bias = biases[width : width + hidden_units]
    mlp_bias = biases[width + hidden_units : 2 * width + hidden_units]
    out_bias = biases[2 * width + hidden_units :]
    thin_count = -(-(channels + 1) // 16) * 16
    spare = thin_count - channels - 1
    encoder = jnp.concatenate(
        [io_weight[0], enc_bias[None], jnp.zeros((spare, width), jnp.float32)], axis=0
    )

    lines = fields.transpose(1, 0, 2).reshape(lat_dev * channels, lon_count)
    lines = jnp.pad(lines, ((0, -lines.shape[0] % 128), (0, 0)))
    spectra = lax.all_gather(dot("rj,psj->psr", lines, forward), "wide", axis=0, tiled=False)

    folded = dot("cd,tpdk->tpck", encoder, spectral_weight)

    my_degrees = lax.dynamic_slice_in_dim(degree_map, position * degree_slots, degree_slots)
    slot_of = jnp.argsort(order_map)
    slots = degree_slots + degree_slots % 2
    if 128 % lat_total == 0 and lax.axis_size("dp") == 4 and wide_count == 8 and lat_total >= 8:
        wire, folded = tables_to_degrees(forward_table, inverse_table, wide_count, degree_slots, folded)
        degrees = jnp.pad(my_degrees, (0, 2 * wire.shape[2] - degree_slots), constant_values=-1)
        own = forward_table.shape[0]
        fwd_rows, inv_rows = table_rows(wire, slot_of, degrees, own, lat_total, slots)
    else:
        fwd_table = lax.all_to_all(forward_table, "wide", split_axis=2, concat_axis=0, tiled=True)
        inv_table = lax.all_to_all(inverse_table, "wide", split_axis=1, concat_axis=0, tiled=True)
        orders = jnp.arange(order_count, dtype=jnp.int32)
        live = (
            (my_degrees[None, :] >= orders[:, None])
            & (orders[:, None] < M)
            & (my_degrees[None, :] < L)
        ).astype(jnp.float32)
        even = ((0, 0), (0, degree_slots % 2), (0, 0), (0, 0))
        fwd_masked = fwd_table[slot_of] * live[:, None, :]
        inv_masked = inv_table[slot_of] * live[:, :, None]
        fwd_masked = fwd_masked.reshape(order_count // 8, 8, lat_total, degree_slots)
        inv_masked = inv_masked.reshape(order_count // 8, 8, degree_slots, lat_total)

        def by_degree(table):
            return jnp.pad(table, even).reshape(order_count // 8, slots, lat_total * 8)

        fwd_rows = by_degree(fwd_masked.transpose(0, 3, 2, 1))
        inv_rows = by_degree(inv_masked.transpose(0, 2, 3, 1))

    grid_coef = spectral_forward(spectra, fwd_rows, inv_rows, folded, lat_dev, channels)
    grid_coef = lax.psum_scatter(grid_coef, "wide", scatter_dimension=0, tiled=True)
    grid_coef = grid_coef.reshape(lat_dev, order_count, 2, width)

    encoded = dot("caj,ck->ajk", fields, io_weight[0]) + enc_bias
    mixed_in = encoded + dot("aspc,psj->ajc", grid_coef, inverse)
    hidden_pre = dot("ajk,kh->ajh", mixed_in, mlp_weight[0]) + hidden_bias
    hidden_act, smooth_back = jax.vjp(smooth, hidden_pre)
    latent = mixed_in + dot("ajh,kh->ajk", hidden_act, mlp_weight[1]) + mlp_bias
    predicted = dot("ajk,ck->caj", latent, io_weight[1]) + out_bias[:, None, None]
    misfit = predicted - truth
    pixel_weight = pixel_weights(land_mask, missing_mask[0], position * lat_dev, lat_total, channels)
    count_local = jnp.sum(pixel_weight)
    weighted = pixel_weight * misfit
    loss_local = jnp.sum(weighted * misfit)
    pred_grad = weighted * (2.0 / entries)
    out_bias_grad = jnp.sum(pred_grad, axis=(1, 2))
    decoder_grad = dot("caj,ajk->ck", pred_grad, latent)
    latent_grad = dot("caj,ck->ajk", pred_grad, io_weight[1])
    mlp_bias_grad = jnp.sum(latent_grad, axis=(0, 1))
    down_grad = dot("ajk,ajh->kh", latent_grad, hidden_act)
    act_grad = dot("ajk,kh->ajh", latent_grad, mlp_weight[1])
    pre_grad = smooth_back(act_grad)[0]
    hidden_bias_grad = jnp.sum(pre_grad, axis=(0, 1))
    up_grad = dot("ajk,ajh->kh", mixed_in, pre_grad)
    mixed_grad = latent_grad + dot("ajh,kh->ajk", pre_grad, mlp_weight[0])

    grid_grad = dot("ajc,psj->aspc", mixed_grad, inverse).reshape(lat_dev, order_count, 2 * width)
    grid_grad = lax.all_gather(grid_grad, "wide", axis=0, tiled=True)
    direct = dot("caj,ajk->ck", fields, mixed_grad)
    direct_bias = jnp.sum(mixed_grad, axis=(0, 1))
    small = [direct_bias, hidden_bias_grad, mlp_bias_grad, out_bias_grad, loss_local[None], count_local[None]]
    small = jnp.concatenate(small)
    small_count = small.shape[0]
    flat = [up_grad.reshape(-1, width), down_grad.reshape(-1, width), decoder_grad, direct]
    flat.append(jnp.pad(small, (0, -small_count % width)).reshape(-1, width))
    flat = jnp.concatenate(flat, axis=0)
    flat = all_sum(jnp.pad(flat, ((0, -flat.shape[0] % 32), (0, 0))))
    grid_grad, flat = lax.optimization_barrier((grid_grad, flat))
    thin = spectral_backward(
        grid_grad, spectra, fwd_rows, inv_rows, degree_slots, thin_count, channels
    )
    at = 2 * hidden_units
    mlp_grad = flat[:at].reshape(2, width, hidden_units)
    decoder_grad = flat[at : at + channels]
    direct = flat[at + channels : at + 2 * channels]
    small = flat[at + 2 * channels :].reshape(-1)[:small_count]
    encoder_grad = all_sum(dot("tpck,tpdk->cd", thin[:degree_slots], spectral_weight))
    gram = jnp.einsum("ck,dk->cd", encoder, encoder, precision=lax.Precision.HIGHEST)
    thin, spectral_squares = thin_sum(thin.reshape(2 * slots, thin_count, width), gram)
    thin = thin.reshape(slots, 2, thin_count, width)
    io_grad = jnp.stack([direct + encoder_grad[:channels], decoder_grad])
    bias_grad = jnp.concatenate([small[:width] + encoder_grad[channels], small[width:-2]])
    loss_sum, valid_weight = small[-2], small[-1]
    rescale = entries / valid_weight
    squares = (
        spectral_squares
        + jnp.sum(io_grad * io_grad)
        + jnp.sum(mlp_grad * mlp_grad)
        + jnp.sum(bias_grad * bias_grad)
    )
    grad_norm = jnp.sqrt(squares) * rescale
    factor = rescale * CLIP_LIMIT / jnp.maximum(grad_norm, CLIP_LIMIT)
    spectral_new, spectral_first_new, spectral_second_new, spectral_low = spectral_adam(
        factor[None], encoder, thin, spectral_weight, spectral_first, spectral_second
    )
    io_new, io_first_new, io_second_new = adam_step(
        io_weight, io_first, io_second, io_grad * factor, WEIGHT_DECAY
    )
    mlp_new, mlp_first_new, mlp_second_new = adam_step(
        mlp_weight, mlp_first, mlp_second, mlp_grad * factor, WEIGHT_DECAY
    )
    bias_new, bias_first_new, bias_second_new = adam_step(
        biases, bias_first, bias_second, bias_grad * factor, 0.0
    )
    return (
        loss_sum,
        valid_weight,
        grad_norm,
        spectral_new,
        spectral_first_new,
        spectral_second_new,
        spectral_low,
        io_new,
        io_first_new,
        io_second_new,
        io_new.astype(jnp.bfloat16),
        mlp_new,
        mlp_first_new,
        mlp_second_new,
        mlp_new.astype(jnp.bfloat16),
        bias_new,
        bias_first_new,
        bias_second_new,
        bias_new.astype(jnp.bfloat16),
    )


def solution(mesh):
    wide4 = P("wide", None, None, None)
    in_specs = (
        P("dp", None, "wide", None),
        P("dp", None, "wide", None),
        P("wide", None),
        P("dp", "wide", None),
        P(),
        P(),
        P("wide", None, None),
        P("wide", None, None),
        wide4,
        wide4,
        wide4,
    ) + (P(),) * 9
    out_specs = (P(),) * 3 + (wide4,) * 4 + (P(),) * 12
    return jax.shard_map(body, mesh=mesh, in_specs=in_specs, out_specs=out_specs, check_vma=False)
```

```python
import functools
import math

import jax
import jax.numpy as jnp
import numpy as np
from jax import lax
from jax.experimental import pallas as pl
from jax.experimental.pallas import tpu as pltpu
from jax.sharding import PartitionSpec as P

M = 360
L = 360
SEA_CH = 1
STEP = 5


HIGH = lax.Precision.HIGH
CLIP_LIMIT = 0.001
LEARN_RATE = 0.1
BETA_ONE = 0.9
BETA_TWO = 0.999
EPSILON = 1e-08
WEIGHT_DECAY = 0.1


def smooth(values):
    return jax.nn.gelu(values, approximate=True)


def dot(spec, left, right):
    return jnp.einsum(spec, left, right, precision=HIGH)


def dft_tables(order_count, lon_count):
    orders = np.arange(order_count, dtype=np.int64)[:, None]
    columns = np.arange(lon_count, dtype=np.int64)[None, :]
    angle = (orders * columns % lon_count) * (2.0 * math.pi / lon_count)
    both = np.stack([np.cos(angle), -np.sin(angle)], axis=0)
    factor = np.where(orders == 0, 1.0, 2.0)[None]
    return (both / lon_count).astype(np.float32), (factor * both).astype(np.float32)


def halves(value):
    high = value.astype(jnp.bfloat16)
    low = (value - high.astype(jnp.float32)).astype(jnp.bfloat16)
    return high, low


def dot3(left, right, dims=(((1,), (0,)), ((), ()))):
    left_high, left_low = halves(left)
    right_high, right_low = halves(right)

    def one(a, b):
        return lax.dot_general(a, b, dims, preferred_element_type=jnp.float32)

    return one(left_high, right_high) + (one(left_high, right_low) + one(left_low, right_high))


def block_diagonal(rows):
    count, lanes = rows.shape
    spread = jnp.broadcast_to(rows[:, None, :], (count, 8, lanes))
    sub = lax.broadcasted_iota(jnp.int32, (count, 8, lanes), 1)
    lane = lax.broadcasted_iota(jnp.int32, (count, 8, lanes), 2) & 7
    return jnp.where(sub == lane, spread, 0.0).reshape(count * 8, lanes)


def steps(count):
    return max(size for size in range(1, 6) if count % size == 0)


def group_rows(group):
    return pl.ds(pl.multiple_of(group * 8, 8), 8)


def legendre(values, table, out_ref, group):
    lat, _, lanes = values.shape
    product = dot3(block_diagonal(table), values.reshape(lat * 8, lanes))
    out_ref[:, group_rows(group), :] = product.reshape(product.shape[0] // 8, 8, lanes)


def channel_spectra(spec_ref, lat_dev, channels, thin, group):
    devices, size, lanes = spec_ref.shape
    spectra = spec_ref[:, group_rows(group), :].reshape(devices * 8, lanes)
    lane = lax.broadcasted_iota(jnp.int32, (devices * 8, lanes), 1)
    order = lax.broadcasted_iota(jnp.int32, (devices * 8, lanes), 0) & 7
    order += pl.program_id(0) * size + group * 8
    ones = jnp.where((order == 0) & (lane == channels), 1.0, 0.0)
    half = thin // 2
    rows = []
    for row in range(lat_dev):
        real = row * channels
        imag = (lat_dev + row) * channels
        left = pltpu.roll(spectra, (lanes - real) % lanes, 1) if row else spectra
        right = pltpu.roll(spectra, (half - imag) % lanes, 1)
        value = jnp.where((lane >= half) & (lane < half + channels), right, ones)
        value = jnp.where(lane < channels, left, value)
        rows.append(value[:, :thin].reshape(devices, 8, thin))
    return jnp.stack(rows, axis=1).reshape(devices * lat_dev, 8, thin)


def forward_kernel(lat_dev, channels, spec_ref, fwd_ref, inv_ref, folded_ref, grid_ref, coef_ref, mixed_ref):
    groups = fwd_ref.shape[0]
    degrees = folded_ref.shape[0]
    slots = mixed_ref.shape[0]
    for spare in range(degrees, slots):
        mixed_ref[spare] = jnp.zeros(mixed_ref.shape[1:], jnp.float32)

    thin = coef_ref.shape[2]

    def analyse(group, carry):
        spectra = channel_spectra(spec_ref, lat_dev, channels, thin, group)
        legendre(spectra, fwd_ref[group], coef_ref, group)
        return carry

    lax.fori_loop(0, groups, analyse, 0, unroll=steps(groups))

    def mix(degree, carry):
        real = folded_ref[degree, 0]
        imag = folded_ref[degree, 1]
        block = jnp.concatenate(
            [jnp.concatenate([real, imag], axis=1), jnp.concatenate([-imag, real], axis=1)], axis=0
        )
        mixed_ref[degree] = dot3(coef_ref[degree], block)
        return carry

    lax.fori_loop(0, degrees, mix, 0, unroll=steps(degrees))

    def synthesise(group, carry):
        rows = pl.ds(pl.multiple_of(group * 8, 8), 8)
        mixed = mixed_ref[:, rows, :]
        product = dot3(
            block_diagonal(inv_ref[group]),
            mixed.reshape(slots * 8, mixed.shape[2]),
            (((0,), (0,)), ((), ())),
        )
        grid_ref[:, rows, :] = product.reshape(product.shape[0] // 8, 8, mixed.shape[2])
        return carry

    lax.fori_loop(0, groups, synthesise, 0, unroll=steps(groups))


def backward_kernel(degrees, lat_dev, fields, grid_ref, spec_ref, fwd_ref, inv_ref, thin_ref, coef_ref, out_ref):
    groups = fwd_ref.shape[0]
    _, _, channels, width = thin_ref.shape

    @pl.when(pl.program_id(0) == 0)
    def _():
        thin_ref[...] = jnp.zeros(thin_ref.shape, jnp.float32)

    def analyse(group, carry):
        spectra = channel_spectra(spec_ref, lat_dev, fields, 2 * channels, group)
        legendre(spectra, fwd_ref[group], coef_ref, group)
        legendre(grid_ref[:, group_rows(group), :], inv_ref[group], out_ref, group)
        return carry

    lax.fori_loop(0, groups, analyse, 0, unroll=steps(groups))

    def product(degree, carry):
        both = dot3(coef_ref[degree], out_ref[degree], (((0,), (0,)), ((), ())))
        thin_ref[degree, 0] += both[:channels, :width] + both[channels:, width:]
        thin_ref[degree, 1] += both[:channels, width:] - both[channels:, :width]
        return carry

    lax.fori_loop(0, degrees, product, 0, unroll=steps(degrees))


def adam_kernel(first_steps, block_ref, thin_block_ref, factor_ref, encoder_ref, *refs):
    one_ref, two_ref, weight_ref, first_ref, second_ref = refs[:5]
    weight_out, first_out, second_out, low_out = refs[-4:]
    factor = factor_ref[0]
    in_one = pl.program_id(0) < first_steps
    encoder_high, encoder_low = halves(encoder_ref[...])
    left = jnp.concatenate([encoder_high, encoder_high, encoder_low], axis=0)
    for degree, part in np.ndindex(one_ref.shape[:2]):
        thin = jnp.where(in_one, one_ref[degree, part], two_ref[degree, part])
        high, low = halves(thin * factor)
        right = jnp.concatenate([high, low, high], axis=0)
        gradient = lax.dot_general(
            left, right, (((0,), (0,)), ((), ())), preferred_element_type=jnp.float32
        )
        weight, first, second = adam_step(
            weight_ref[degree, part], first_ref[degree, part], second_ref[degree, part], gradient, WEIGHT_DECAY
        )
        weight_out[degree, part] = weight
        first_out[degree, part] = first
        second_out[degree, part] = second
        low_out[degree, part] = weight.astype(jnp.bfloat16)


def table_kernel(own, me_ref, slot_ref, wire_ref, degree_ref, place_ref, *rows_refs):
    groups, slots, lanes = rows_refs[0].shape
    lat = lanes // 8
    per_tile = 128 // lat
    degree = degree_ref[...]
    count = degree.shape[0]
    lane = lax.broadcasted_iota(jnp.int32, (count, 128), 1) // lat
    me = me_ref[0]
    me_wide = me_ref[1]

    def one_group(group, carry):
        found = ([], [])
        for first in range(0, 8, per_tile):
            tiles = [jnp.zeros((count, 128), jnp.float32)] * 2
            for place in range(per_tile):
                order = group * 8 + first + place
                slot = slot_ref[order]
                source = slot // own
                at = slot - source * own
                block = at // per_tile
                columns = pl.ds(pl.multiple_of(block * 128, 128), 128)
                shift = lax.rem((place - (at - block * per_tile)) * lat + 128, 128)
                live = (degree >= order) & (order < M) & (degree < L) & (lane == place)
                for table in range(2):
                    both = [wire_ref[(2 * table + half) ^ me, source ^ me_wide, :, columns] for half in range(2)]
                    moved = pltpu.roll(jnp.concatenate(both, axis=0), shift, 1)
                    tiles[table] = jnp.where(live, moved, tiles[table])
            for table in range(2):
                found[table].append(tiles[table])
        place = place_ref[...]
        for table in range(2):
            high, low = halves(jnp.concatenate(found[table], axis=1))
            rows = jnp.dot(high, place, preferred_element_type=jnp.float32)
            rows += jnp.dot(low, place, preferred_element_type=jnp.float32)
            rows_refs[table][group] = rows[:slots]
        return carry

    lax.fori_loop(0, groups, one_group, 0, unroll=steps(groups))


def order_chunk(order_count, lat_total, width):
    best = 8
    for size in range(8, order_count + 1, 8):
        if order_count % size == 0 and lat_total * size * width * 8 <= 8.5 * 2**20:
            best = size
    return best


def vmem(mebibytes):
    return pltpu.CompilerParams(
        dimension_semantics=("arbitrary",), vmem_limit_bytes=mebibytes * 2**20
    )


def table_rows(wire, slot_of, degrees, own, lat_total, slots):
    groups = slot_of.shape[0] // 8
    lane = np.arange(lat_total * 8)
    place = np.zeros((lat_total * 8, lat_total * 8), np.float32)
    place[lane, lane % lat_total * 8 + lane // lat_total] = 1.0
    return pl.pallas_call(
        functools.partial(table_kernel, own),
        in_specs=[pl.BlockSpec(memory_space=pltpu.SMEM)] * 2
        + [pl.BlockSpec(memory_space=pltpu.VMEM)] * 3,
        out_specs=[pl.BlockSpec(memory_space=pltpu.VMEM)] * 2,
        out_shape=[jax.ShapeDtypeStruct((groups, slots, lat_total * 8), jnp.float32)] * 2,
        compiler_params=pltpu.CompilerParams(vmem_limit_bytes=32 * 2**20),
        name="table_rows",
    )(jnp.stack([lax.axis_index("dp"), lax.axis_index("wide")]), slot_of, wire, degrees[:, None], jnp.asarray(place, jnp.bfloat16))


def exchange(value, axis, count, bit):
    return lax.ppermute(value, axis, [(i, i ^ bit) for i in range(count)])


def wire_kernel(degrees, me_ref, forward_ref, inverse_ref, wire_ref, turned_ref):
    own, lat, order_count = forward_ref.shape
    owners, half, lanes = wire_ref.shape
    per_tile = 128 // lat
    me = me_ref[0]

    @pl.when(me < 2)
    def _():
        turned_ref[order_count:] = jnp.zeros((turned_ref.shape[0] - order_count, lanes), jnp.float32)
        turned_ref[:order_count, : own * lat] = forward_ref[...].reshape(own * lat, order_count).T
        if lanes > own * lat:
            turned_ref[:order_count, own * lat :] = jnp.zeros(
                (order_count, lanes - own * lat), jnp.float32
            )

    def forward_part(part):
        for owner in range(owners):
            first = owner * degrees + part * half
            wire_ref[owner] = turned_ref[first : first + half, :]

    def inverse_part(part):
        lane = lax.broadcasted_iota(jnp.int32, (half, 128), 1) // lat
        for owner in range(owners):
            first = owner * degrees + part * half
            rows = min(half, order_count - first)
            for tile in range(lanes // 128):
                value = jnp.zeros((rows, 128), jnp.float32)
                for place in range(per_tile):
                    slot = tile * per_tile + place
                    if slot < own:
                        found = inverse_ref[slot, first : first + rows, :]
                        found = jnp.concatenate([found] * per_tile, axis=1)
                        value = jnp.where(lane[:rows] == place, found, value)
                columns = slice(tile * 128, tile * 128 + 128)
                wire_ref[owner, :rows, columns] = value
                if rows < half:
                    wire_ref[owner, rows:, columns] = jnp.zeros((half - rows, 128), jnp.float32)

    pl.when(me == 0)(functools.partial(forward_part, 0))
    pl.when(me == 1)(functools.partial(forward_part, 1))
    pl.when(me == 2)(functools.partial(inverse_part, 0))
    pl.when(me == 3)(functools.partial(inverse_part, 1))


def tables_to_degrees(forward_table, inverse_table, wide_count, degree_slots, beside):
    own, lat_total, order_count = forward_table.shape
    dp_count = lax.axis_size("dp")
    half = -(-degree_slots // 16) * 8
    lanes = -(-own * lat_total // 128) * 128
    wire = pl.pallas_call(
        functools.partial(wire_kernel, degree_slots),
        in_specs=[pl.BlockSpec(memory_space=pltpu.SMEM)]
        + [pl.BlockSpec(memory_space=pltpu.VMEM)] * 2,
        out_specs=pl.BlockSpec(memory_space=pltpu.VMEM),
        out_shape=jax.ShapeDtypeStruct((wide_count, half, lanes), jnp.float32),
        scratch_shapes=[pltpu.VMEM((order_count + 2 * half - degree_slots + 8, lanes), jnp.float32)],
        compiler_params=pltpu.CompilerParams(vmem_limit_bytes=32 * 2**20),
        name="table_wire",
    )(lax.axis_index("dp")[None], forward_table, inverse_table)
    me = lax.axis_index("wide")
    pieces = [lax.dynamic_index_in_dim(wire, me ^ k, 0, keepdims=False) for k in range(wide_count)]
    pieces = [pieces[0]] + [exchange(pieces[k], "wide", wide_count, k) for k in range(1, wide_count)]
    wire, beside = lax.optimization_barrier((jnp.stack(pieces), beside))
    found = []
    for part, bits in ((wire[: wide_count // 2], (1, 2)), (wire[wide_count // 2 :], (2, 1))):
        by_index = {0: part}
        for bit in bits:
            names = list(by_index)
            passed = exchange(jnp.stack([by_index[i] for i in names]), "dp", dp_count, bit)
            by_index.update({i ^ bit: passed[k] for k, i in enumerate(names)})
        found.append(jnp.stack([by_index[i] for i in range(4)]))
    return jnp.concatenate(found, axis=1), beside


def reduce_halves(piece, bits):
    me = lax.axis_index("dp")
    for bit in bits:
        parts = piece.reshape((2, piece.shape[0] // 2) + piece.shape[1:])
        mine = (me & bit) // bit
        sent = lax.dynamic_index_in_dim(parts, 1 - mine, 0, keepdims=False)
        kept = lax.dynamic_index_in_dim(parts, mine, 0, keepdims=False)
        piece = kept + exchange(sent, "dp", 4, bit)
    return piece


def gather_half(piece, bit):
    other = exchange(piece, "dp", 4, bit)
    low = lax.axis_index("dp") & bit == 0
    return jnp.concatenate([jnp.where(low, piece, other), jnp.where(low, other, piece)], axis=0)


def gather_halves(piece, bits):
    for bit in bits[::-1]:
        piece = gather_half(piece, bit)
    return piece


def wide_sum(piece):
    wide_count = lax.axis_size("wide")
    bit = 1
    while bit < wide_count:
        piece = piece + exchange(piece, "wide", wide_count, bit)
        bit *= 2
    return piece


def by_bits():
    wide_count = lax.axis_size("wide")
    return lax.axis_size("dp") == 4 and wide_count & (wide_count - 1) == 0


def all_sum(rows):
    if not by_bits():
        return lax.psum(rows, ("dp", "wide"))
    return gather_halves(wide_sum(reduce_halves(rows, (1, 2))), (1, 2))


def thin_sum(thin, gram, cut):
    def squares(piece):
        product = jnp.einsum("cd,tdk->tck", gram, piece, precision=lax.Precision.HIGHEST)
        return jnp.sum(piece * product)

    me = lax.axis_index("dp")
    if not by_bits():
        thin = lax.psum(thin, "dp")
        parts = []
        for part in (thin[:cut], thin[cut:]):
            middle = part.shape[0] // 2
            parts.append((part[:middle], part[middle:], True))
        return parts, lax.psum(squares(thin), "wide")
    one, two = reduce_halves(thin[:cut], (1, 2)), reduce_halves(thin[cut:], (2, 1))
    total = jnp.broadcast_to(squares(one) + squares(two), (8, 128))
    for bit in (1, 2):
        total = total + exchange(total, "dp", 4, bit)
    total = wide_sum(total)[0, 0]
    one, two = gather_half(one, 2), gather_half(two, 1)
    parts = [
        (one, exchange(one, "dp", 4, 1), me & 1 == 0),
        (two, exchange(two, "dp", 4, 2), me & 2 == 0),
    ]
    return parts, total


def spectral_forward(spectra, fwd_rows, inv_rows, folded, lat_dev, fields):
    devices, order_count, lanes = spectra.shape
    lat_total = devices * lat_dev
    degrees, _, channels, width = folded.shape
    thin = 2 * channels
    slots = fwd_rows.shape[1]
    size = order_chunk(order_count, lat_total, width)
    groups = size // 8
    return pl.pallas_call(
        functools.partial(forward_kernel, lat_dev, fields),
        grid=(order_count // size,),
        in_specs=[
            pl.BlockSpec((devices, size, lanes), lambda i: (0, i, 0)),
            pl.BlockSpec((groups,) + fwd_rows.shape[1:], lambda i: (i, 0, 0)),
            pl.BlockSpec((groups,) + inv_rows.shape[1:], lambda i: (i, 0, 0)),
            pl.BlockSpec(folded.shape, lambda i: (0, 0, 0, 0)),
        ],
        out_specs=pl.BlockSpec((lat_total, size, 2 * width), lambda i: (0, i, 0)),
        out_shape=jax.ShapeDtypeStruct((lat_total, order_count, 2 * width), jnp.float32),
        scratch_shapes=[
            pltpu.VMEM((slots, size, thin), jnp.float32),
            pltpu.VMEM((slots, size, 2 * width), jnp.float32),
        ],
        compiler_params=vmem(60),
        name="spectral_forward",
    )(spectra, fwd_rows, inv_rows, folded)


def spectral_backward(grid_grad, spectra, fwd_rows, inv_rows, degrees, channels, fields):
    devices, order_count, lanes = spectra.shape
    lat_total = grid_grad.shape[0]
    lat_dev = lat_total // devices
    thin = 2 * channels
    block, first_steps, second_steps = adam_split(degrees)
    thin_slots = 2 * block * (first_steps + second_steps)
    width = grid_grad.shape[2] // 2
    slots = fwd_rows.shape[1]
    size = order_chunk(order_count, lat_total, width)
    groups = size // 8
    table = pl.BlockSpec((groups,) + fwd_rows.shape[1:], lambda i: (i, 0, 0))
    return pl.pallas_call(
        functools.partial(backward_kernel, degrees, lat_dev, fields),
        grid=(order_count // size,),
        in_specs=[
            pl.BlockSpec((lat_total, size, 2 * width), lambda i: (0, i, 0)),
            pl.BlockSpec((devices, size, lanes), lambda i: (0, i, 0)),
            table,
            table,
        ],
        out_specs=pl.BlockSpec((thin_slots, 2, channels, width), lambda i: (0, 0, 0, 0)),
        out_shape=jax.ShapeDtypeStruct((thin_slots, 2, channels, width), jnp.float32),
        scratch_shapes=[
            pltpu.VMEM((slots, size, thin), jnp.float32),
            pltpu.VMEM((slots, size, 2 * width), jnp.float32),
        ],
        compiler_params=vmem(60),
        name="spectral_backward",
    )(grid_grad, spectra, fwd_rows, inv_rows)


def adam_split(degrees):
    size = 3 if degrees % 3 == 0 and degrees >= 12 else 1
    steps_all = -(-degrees // (2 * size))
    return size, steps_all // 2, steps_all - steps_all // 2


def spectral_adam(factor, encoder, one, two, low_one, low_two, weights, done):
    weight = weights[0]
    degrees = weight.shape[0]
    size, first_steps, second_steps = adam_split(degrees)
    step = jnp.arange(first_steps + second_steps, dtype=jnp.int32)
    start_two = 2 * first_steps + jnp.where(low_two, 0, second_steps)
    block = jnp.where(
        step < first_steps, step + jnp.where(low_one, 0, first_steps), step - first_steps + start_two
    )
    block = jnp.minimum(block, degrees // size - 1)
    thin_block = jnp.where(step < first_steps, 0, block - start_two)
    whole = pl.BlockSpec((size,) + weight.shape[1:], lambda i, b, t: (b[i], 0, 0, 0))
    thin = (size,) + one.shape[1:]
    outs = [jax.ShapeDtypeStruct(weight.shape, jnp.float32)] * 3
    outs.append(jax.ShapeDtypeStruct(weight.shape, jnp.bfloat16))
    return pl.pallas_call(
        functools.partial(adam_kernel, first_steps),
        grid_spec=pltpu.PrefetchScalarGridSpec(
            num_scalar_prefetch=2,
            grid=(first_steps + second_steps,),
            in_specs=[
                pl.BlockSpec(memory_space=pltpu.SMEM),
                pl.BlockSpec(encoder.shape, lambda i, b, t: (0, 0)),
                pl.BlockSpec(thin, lambda i, b, t: (jnp.minimum(i, first_steps - 1), 0, 0, 0)),
                pl.BlockSpec(thin, lambda i, b, t: (t[i], 0, 0, 0)),
                whole,
                whole,
                whole,
            ]
            + [pl.BlockSpec(memory_space=pl.ANY)] * len(done),
            out_specs=[whole] * 4,
        ),
        out_shape=outs,
        input_output_aliases={9 + k: k for k in range(len(done))},
        compiler_params=vmem(48),
        name="spectral_adam",
    )(block, thin_block, factor, encoder, one, two, *weights, *done)


def pixel_weights(land_mask, missing_rows, first_row, lat_total, channels):
    lat_dev = land_mask.shape[0]
    latitude = (first_row + jnp.arange(lat_dev, dtype=jnp.int32)).astype(jnp.float32)
    cos_lat = jnp.sin(math.pi * (latitude + 0.5) / lat_total)
    sea_part = (1 - land_mask).astype(jnp.float32)
    valid_part = (1 - missing_rows).astype(jnp.float32) * cos_lat[:, None]
    sea_only = (jnp.arange(channels, dtype=jnp.int32) < SEA_CH)[:, None, None]
    return jnp.where(sea_only, sea_part[None], 1.0) * valid_part[None]


def adam_step(weight, moment_one, moment_two, gradient, decay_rate):
    first_new = BETA_ONE * moment_one + (1.0 - BETA_ONE) * gradient
    second_new = BETA_TWO * moment_two + (1.0 - BETA_TWO) * gradient * gradient
    first_hat = first_new * (1.0 / (1.0 - BETA_ONE**STEP))
    second_hat = second_new * (1.0 / (1.0 - BETA_TWO**STEP))
    weight_new = weight - LEARN_RATE * (
        first_hat / (jnp.sqrt(second_hat) + EPSILON) + decay_rate * weight
    )
    return (weight_new, first_new, second_new)


def body(
    inputs,
    targets,
    land_mask,
    missing_mask,
    order_map,
    degree_map,
    forward_table,
    inverse_table,
    spectral_weight,
    spectral_first,
    spectral_second,
    io_weight,
    io_first,
    io_second,
    mlp_weight,
    mlp_first,
    mlp_second,
    biases,
    bias_first,
    bias_second,
):
    fields = inputs[0]
    truth = targets[0]
    lat_dev = fields.shape[1]
    lon_count = fields.shape[2]
    channels = io_weight.shape[1]
    width = io_weight.shape[2]
    hidden_units = mlp_weight.shape[2]
    wide_count = lax.axis_size("wide")
    position = lax.axis_index("wide")
    order_count = order_map.shape[0]
    degree_slots = spectral_weight.shape[0]
    lat_total = lat_dev * wide_count
    entries = lax.axis_size("dp") * channels * lat_total * lon_count
    forward, inverse = dft_tables(order_count, lon_count)

    enc_bias = biases[:width]
    hidden_bias = biases[width : width + hidden_units]
    mlp_bias = biases[width + hidden_units : 2 * width + hidden_units]
    out_bias = biases[2 * width + hidden_units :]
    thin_count = -(-(channels + 1) // 16) * 16
    spare = thin_count - channels - 1
    encoder = jnp.concatenate(
        [io_weight[0], enc_bias[None], jnp.zeros((spare, width), jnp.float32)], axis=0
    )

    lines = fields.transpose(1, 0, 2).reshape(lat_dev * channels, lon_count)
    spectra = [dot("rj,sj->sr", lines, table) for table in forward]
    spare = -2 * lat_dev * channels % 128
    spectra = jnp.concatenate(spectra + [jnp.zeros((order_count, spare), jnp.float32)], axis=1)

    folded = dot("cd,tpdk->tpck", encoder, spectral_weight)

    my_degrees = lax.dynamic_slice_in_dim(degree_map, position * degree_slots, degree_slots)
    slot_of = jnp.argsort(order_map)
    slots = degree_slots + degree_slots % 2
    if 128 % lat_total == 0 and lax.axis_size("dp") == 4 and wide_count == 8 and lat_total >= 8:
        wire, (folded, spectra) = tables_to_degrees(
            forward_table, inverse_table, wide_count, degree_slots, (folded, spectra)
        )
        degrees = jnp.pad(my_degrees, (0, 2 * wire.shape[2] - degree_slots), constant_values=-1)
        own = forward_table.shape[0]
        fwd_rows, inv_rows = table_rows(wire, slot_of, degrees, own, lat_total, slots)
    else:
        fwd_table = lax.all_to_all(forward_table, "wide", split_axis=2, concat_axis=0, tiled=True)
        inv_table = lax.all_to_all(inverse_table, "wide", split_axis=1, concat_axis=0, tiled=True)
        orders = jnp.arange(order_count, dtype=jnp.int32)
        live = (
            (my_degrees[None, :] >= orders[:, None])
            & (orders[:, None] < M)
            & (my_degrees[None, :] < L)
        ).astype(jnp.float32)
        even = ((0, 0), (0, degree_slots % 2), (0, 0), (0, 0))
        fwd_masked = fwd_table[slot_of] * live[:, None, :]
        inv_masked = inv_table[slot_of] * live[:, :, None]
        fwd_masked = fwd_masked.reshape(order_count // 8, 8, lat_total, degree_slots)
        inv_masked = inv_masked.reshape(order_count // 8, 8, degree_slots, lat_total)

        def by_degree(table):
            return jnp.pad(table, even).reshape(order_count // 8, slots, lat_total * 8)

        fwd_rows = by_degree(fwd_masked.transpose(0, 3, 2, 1))
        inv_rows = by_degree(inv_masked.transpose(0, 2, 3, 1))

    spectra = lax.all_gather(spectra, "wide", axis=0, tiled=False)
    grid_coef = spectral_forward(spectra, fwd_rows, inv_rows, folded, lat_dev, channels)
    grid_coef = lax.psum_scatter(grid_coef, "wide", scatter_dimension=0, tiled=True)
    grid_coef = grid_coef.reshape(lat_dev, order_count, 2, width)

    encoded = dot("caj,ck->ajk", fields, io_weight[0]) + enc_bias
    mixed_in = encoded + dot("aspc,psj->ajc", grid_coef, inverse)
    hidden_pre = dot("ajk,kh->ajh", mixed_in, mlp_weight[0]) + hidden_bias
    hidden_act, smooth_back = jax.vjp(smooth, hidden_pre)
    latent = mixed_in + dot("ajh,kh->ajk", hidden_act, mlp_weight[1]) + mlp_bias
    predicted = dot("ajk,ck->caj", latent, io_weight[1]) + out_bias[:, None, None]
    misfit = predicted - truth
    pixel_weight = pixel_weights(land_mask, missing_mask[0], position * lat_dev, lat_total, channels)
    count_local = jnp.sum(pixel_weight)
    weighted = pixel_weight * misfit
    loss_local = jnp.sum(weighted * misfit)
    pred_grad = weighted * (2.0 / entries)
    out_bias_grad = jnp.sum(pred_grad, axis=(1, 2))
    decoder_grad = dot("caj,ajk->ck", pred_grad, latent)
    latent_grad = dot("caj,ck->ajk", pred_grad, io_weight[1])
    mlp_bias_grad = jnp.sum(latent_grad, axis=(0, 1))
    down_grad = dot("ajk,ajh->kh", latent_grad, hidden_act)
    act_grad = dot("ajk,kh->ajh", latent_grad, mlp_weight[1])
    pre_grad = smooth_back(act_grad)[0]
    hidden_bias_grad = jnp.sum(pre_grad, axis=(0, 1))
    up_grad = dot("ajk,ajh->kh", mixed_in, pre_grad)
    mixed_grad = latent_grad + dot("ajh,kh->ajk", pre_grad, mlp_weight[0])

    grid_grad = dot("ajc,psj->aspc", mixed_grad, inverse).reshape(lat_dev, order_count, 2 * width)
    grid_grad = lax.all_gather(grid_grad, "wide", axis=0, tiled=True)
    direct = dot("caj,ajk->ck", fields, mixed_grad)
    direct_bias = jnp.sum(mixed_grad, axis=(0, 1))
    small = [direct_bias, hidden_bias_grad, mlp_bias_grad, out_bias_grad, loss_local[None], count_local[None]]
    small = jnp.concatenate(small)
    small_count = small.shape[0]
    flat = [up_grad.reshape(-1, width), down_grad.reshape(-1, width), decoder_grad, direct]
    flat.append(jnp.pad(small, (0, -small_count % width)).reshape(-1, width))
    flat = jnp.concatenate(flat, axis=0)
    flat = all_sum(jnp.pad(flat, ((0, -flat.shape[0] % 32), (0, 0))))
    grid_grad, flat = lax.optimization_barrier((grid_grad, flat))
    thin = spectral_backward(
        grid_grad, spectra, fwd_rows, inv_rows, degree_slots, thin_count, channels
    )
    at = 2 * hidden_units
    mlp_grad = flat[:at].reshape(2, width, hidden_units)
    decoder_grad = flat[at : at + channels]
    direct = flat[at + channels : at + 2 * channels]
    small = flat[at + 2 * channels :].reshape(-1)[:small_count]
    encoder_grad = all_sum(dot("tpck,tpdk->cd", thin[:degree_slots], spectral_weight))
    gram = jnp.einsum("ck,dk->cd", encoder, encoder, precision=lax.Precision.HIGHEST)
    size, first_steps, _ = adam_split(degree_slots)
    pairs = thin.reshape((-1,) + thin.shape[2:])
    parts, spectral_squares = thin_sum(pairs, gram, 4 * size * first_steps)
    io_grad = jnp.stack([direct + encoder_grad[:channels], decoder_grad])
    bias_grad = jnp.concatenate([small[:width] + encoder_grad[channels], small[width:-2]])
    loss_sum, valid_weight = small[-2], small[-1]
    rescale = entries / valid_weight
    squares = (
        spectral_squares
        + jnp.sum(io_grad * io_grad)
        + jnp.sum(mlp_grad * mlp_grad)
        + jnp.sum(bias_grad * bias_grad)
    )
    grad_norm = jnp.sqrt(squares) * rescale
    factor = rescale * CLIP_LIMIT / jnp.maximum(grad_norm, CLIP_LIMIT)
    spectral = ()
    weights = (spectral_weight, spectral_first, spectral_second)
    for half in range(2):
        one, two = (part[half].reshape((-1, 2) + thin.shape[2:]) for part in parts)
        low_one, low_two = ((part[2] if half == 0 else jnp.logical_not(part[2])) for part in parts)
        spectral = spectral_adam(factor[None], encoder, one, two, low_one, low_two, weights, spectral)
    spectral_new, spectral_first_new, spectral_second_new, spectral_low = spectral
    io_new, io_first_new, io_second_new = adam_step(
        io_weight, io_first, io_second, io_grad * factor, WEIGHT_DECAY
    )
    mlp_new, mlp_first_new, mlp_second_new = adam_step(
        mlp_weight, mlp_first, mlp_second, mlp_grad * factor, WEIGHT_DECAY
    )
    bias_new, bias_first_new, bias_second_new = adam_step(
        biases, bias_first, bias_second, bias_grad * factor, 0.0
    )
    return (
        loss_sum,
        valid_weight,
        grad_norm,
        spectral_new,
        spectral_first_new,
        spectral_second_new,
        spectral_low,
        io_new,
        io_first_new,
        io_second_new,
        io_new.astype(jnp.bfloat16),
        mlp_new,
        mlp_first_new,
        mlp_second_new,
        mlp_new.astype(jnp.bfloat16),
        bias_new,
        bias_first_new,
        bias_second_new,
        bias_new.astype(jnp.bfloat16),
    )


def solution(mesh):
    wide4 = P("wide", None, None, None)
    in_specs = (
        P("dp", None, "wide", None),
        P("dp", None, "wide", None),
        P("wide", None),
        P("dp", "wide", None),
        P(),
        P(),
        P("wide", None, None),
        P("wide", None, None),
        wide4,
        wide4,
        wide4,
    ) + (P(),) * 9
    out_specs = (P(),) * 3 + (wide4,) * 4 + (P(),) * 12
    return jax.shard_map(body, mesh=mesh, in_specs=in_specs, out_specs=out_specs, check_vma=False)
```

```python
import functools
import math

import jax
import jax.numpy as jnp
import numpy as np
from jax import lax
from jax.experimental import pallas as pl
from jax.experimental.pallas import tpu as pltpu
from jax.sharding import PartitionSpec as P

M = 360
L = 360
SEA_CH = 1
STEP = 5


HIGH = lax.Precision.HIGH
CLIP_LIMIT = 0.001
LEARN_RATE = 0.1
BETA_ONE = 0.9
BETA_TWO = 0.999
EPSILON = 1e-08
WEIGHT_DECAY = 0.1


def smooth(values):
    return jax.nn.gelu(values, approximate=True)


def dot(spec, left, right):
    return jnp.einsum(spec, left, right, precision=HIGH)


def dft_tables(order_count, lon_count):
    orders = np.arange(order_count, dtype=np.int64)[:, None]
    columns = np.arange(lon_count, dtype=np.int64)[None, :]
    angle = (orders * columns % lon_count) * (2.0 * math.pi / lon_count)
    both = np.stack([np.cos(angle), -np.sin(angle)], axis=0)
    factor = np.where(orders == 0, 1.0, 2.0)[None]
    return (both / lon_count).astype(np.float32), (factor * both).astype(np.float32)


def halves(value):
    high = value.astype(jnp.bfloat16)
    low = (value - high.astype(jnp.float32)).astype(jnp.bfloat16)
    return high, low


def dot3(left, right, dims=(((1,), (0,)), ((), ()))):
    left_high, left_low = halves(left)
    right_high, right_low = halves(right)

    def one(a, b):
        return lax.dot_general(a, b, dims, preferred_element_type=jnp.float32)

    return one(left_high, right_high) + (one(left_high, right_low) + one(left_low, right_high))


def block_diagonal(rows):
    count, lanes = rows.shape
    spread = jnp.broadcast_to(rows[:, None, :], (count, 8, lanes))
    sub = lax.broadcasted_iota(jnp.int32, (count, 8, lanes), 1)
    lane = lax.broadcasted_iota(jnp.int32, (count, 8, lanes), 2) & 7
    return jnp.where(sub == lane, spread, 0.0).reshape(count * 8, lanes)


def steps(count):
    return max(size for size in range(1, 16) if count % size == 0)


def group_rows(group):
    return pl.ds(pl.multiple_of(group * 8, 8), 8)


def legendre(values, table, out_ref, group):
    lat, _, lanes = values.shape
    product = dot3(block_diagonal(table), values.reshape(lat * 8, lanes))
    out_ref[:, group_rows(group), :] = product.reshape(product.shape[0] // 8, 8, lanes)


def channel_spectra(spec_ref, lat_dev, channels, thin, group):
    devices, size, lanes = spec_ref.shape
    spectra = spec_ref[:, group_rows(group), :].reshape(devices * 8, lanes)
    lane = lax.broadcasted_iota(jnp.int32, (devices * 8, lanes), 1)
    order = lax.broadcasted_iota(jnp.int32, (devices * 8, lanes), 0) & 7
    order += pl.program_id(0) * size + group * 8
    ones = jnp.where((order == 0) & (lane == channels), 1.0, 0.0)
    half = thin // 2
    rows = []
    for row in range(lat_dev):
        real = row * channels
        imag = (lat_dev + row) * channels
        left = pltpu.roll(spectra, (lanes - real) % lanes, 1) if row else spectra
        right = pltpu.roll(spectra, (half - imag) % lanes, 1)
        value = jnp.where((lane >= half) & (lane < half + channels), right, ones)
        value = jnp.where(lane < channels, left, value)
        rows.append(value[:, :thin].reshape(devices, 8, thin))
    return jnp.stack(rows, axis=1).reshape(devices * lat_dev, 8, thin)


def forward_kernel(lat_dev, channels, spec_ref, fwd_ref, inv_ref, folded_ref, grid_ref, coef_ref, mixed_ref):
    groups = fwd_ref.shape[0]
    degrees = folded_ref.shape[0]
    slots = mixed_ref.shape[0]
    for spare in range(degrees, slots):
        mixed_ref[spare] = jnp.zeros(mixed_ref.shape[1:], jnp.float32)

    thin = coef_ref.shape[2]

    def analyse(group, carry):
        spectra = channel_spectra(spec_ref, lat_dev, channels, thin, group)
        legendre(spectra, fwd_ref[group], coef_ref, group)
        return carry

    lax.fori_loop(0, groups, analyse, 0, unroll=steps(groups))

    def mix(degree, carry):
        real = folded_ref[degree, 0]
        imag = folded_ref[degree, 1]
        block = jnp.concatenate(
            [jnp.concatenate([real, imag], axis=1), jnp.concatenate([-imag, real], axis=1)], axis=0
        )
        mixed_ref[degree] = dot3(coef_ref[degree], block)
        return carry

    lax.fori_loop(0, degrees, mix, 0, unroll=steps(degrees))

    def synthesise(group, carry):
        rows = pl.ds(pl.multiple_of(group * 8, 8), 8)
        mixed = mixed_ref[:, rows, :]
        product = dot3(
            block_diagonal(inv_ref[group]),
            mixed.reshape(slots * 8, mixed.shape[2]),
            (((0,), (0,)), ((), ())),
        )
        grid_ref[:, rows, :] = product.reshape(product.shape[0] // 8, 8, mixed.shape[2])
        return carry

    lax.fori_loop(0, groups, synthesise, 0, unroll=steps(groups))


def backward_kernel(degrees, lat_dev, fields, grid_ref, spec_ref, fwd_ref, inv_ref, thin_ref, coef_ref, out_ref):
    groups = fwd_ref.shape[0]
    _, _, channels, width = thin_ref.shape

    @pl.when(pl.program_id(0) == 0)
    def _():
        thin_ref[...] = jnp.zeros(thin_ref.shape, jnp.float32)

    def analyse(group, carry):
        spectra = channel_spectra(spec_ref, lat_dev, fields, 2 * channels, group)
        legendre(spectra, fwd_ref[group], coef_ref, group)
        legendre(grid_ref[:, group_rows(group), :], inv_ref[group], out_ref, group)
        return carry

    lax.fori_loop(0, groups, analyse, 0, unroll=steps(groups))

    def product(degree, carry):
        both = dot3(coef_ref[degree], out_ref[degree], (((0,), (0,)), ((), ())))
        thin_ref[degree, 0] += both[:channels, :width] + both[channels:, width:]
        thin_ref[degree, 1] += both[:channels, width:] - both[channels:, :width]
        return carry

    lax.fori_loop(0, degrees, product, 0, unroll=steps(degrees))


def adam_kernel(first_steps, block_ref, thin_block_ref, factor_ref, encoder_ref, *refs):
    one_ref, two_ref, weight_ref, first_ref, second_ref = refs[:5]
    weight_out, first_out, second_out, low_out = refs[-4:]
    factor = factor_ref[0]
    in_one = pl.program_id(0) < first_steps
    encoder_high, encoder_low = halves(encoder_ref[...])
    left = jnp.concatenate([encoder_high, encoder_high, encoder_low], axis=0)
    for degree, part in np.ndindex(one_ref.shape[:2]):
        thin = jnp.where(in_one, one_ref[degree, part], two_ref[degree, part])
        high, low = halves(thin * factor)
        right = jnp.concatenate([high, low, high], axis=0)
        gradient = lax.dot_general(
            left, right, (((0,), (0,)), ((), ())), preferred_element_type=jnp.float32
        )
        weight, first, second = adam_step(
            weight_ref[degree, part], first_ref[degree, part], second_ref[degree, part], gradient, WEIGHT_DECAY
        )
        weight_out[degree, part] = weight
        first_out[degree, part] = first
        second_out[degree, part] = second
        low_out[degree, part] = weight.astype(jnp.bfloat16)


def table_kernel(own, me_ref, slot_ref, wire_ref, degree_ref, place_ref, *rows_refs):
    groups, slots, lanes = rows_refs[0].shape
    lat = lanes // 8
    per_tile = 128 // lat
    degree = degree_ref[...]
    count = degree.shape[0]
    lane = lax.broadcasted_iota(jnp.int32, (count, 128), 1) // lat
    me = me_ref[0]
    me_wide = me_ref[1]

    def one_group(group, carry):
        found = ([], [])
        for first in range(0, 8, per_tile):
            tiles = [jnp.zeros((count, 128), jnp.float32)] * 2
            for place in range(per_tile):
                order = group * 8 + first + place
                slot = slot_ref[order]
                source = slot // own
                at = slot - source * own
                block = at // per_tile
                columns = pl.ds(pl.multiple_of(block * 128, 128), 128)
                shift = lax.rem((place - (at - block * per_tile)) * lat + 128, 128)
                live = (degree >= order) & (order < M) & (degree < L) & (lane == place)
                for table in range(2):
                    both = [wire_ref[(2 * table + half) ^ me, source ^ me_wide, :, columns] for half in range(2)]
                    moved = pltpu.roll(jnp.concatenate(both, axis=0), shift, 1)
                    tiles[table] = jnp.where(live, moved, tiles[table])
            for table in range(2):
                found[table].append(tiles[table])
        place = place_ref[...]
        for table in range(2):
            high, low = halves(jnp.concatenate(found[table], axis=1))
            rows = jnp.dot(high, place, preferred_element_type=jnp.float32)
            rows += jnp.dot(low, place, preferred_element_type=jnp.float32)
            rows_refs[table][group] = rows[:slots]
        return carry

    lax.fori_loop(0, groups, one_group, 0, unroll=steps(groups))


def order_chunk(order_count, lat_total, width):
    best = 8
    for size in range(8, order_count + 1, 8):
        if order_count % size == 0 and lat_total * size * width * 8 <= 8.5 * 2**20:
            best = size
    return best


def vmem(mebibytes):
    return pltpu.CompilerParams(
        dimension_semantics=("arbitrary",), vmem_limit_bytes=mebibytes * 2**20
    )


def table_rows(wire, slot_of, degrees, own, lat_total, slots):
    groups = slot_of.shape[0] // 8
    lane = np.arange(lat_total * 8)
    place = np.zeros((lat_total * 8, lat_total * 8), np.float32)
    place[lane, lane % lat_total * 8 + lane // lat_total] = 1.0
    return pl.pallas_call(
        functools.partial(table_kernel, own),
        in_specs=[pl.BlockSpec(memory_space=pltpu.SMEM)] * 2
        + [pl.BlockSpec(memory_space=pltpu.VMEM)] * 3,
        out_specs=[pl.BlockSpec(memory_space=pltpu.VMEM)] * 2,
        out_shape=[jax.ShapeDtypeStruct((groups, slots, lat_total * 8), jnp.float32)] * 2,
        compiler_params=pltpu.CompilerParams(vmem_limit_bytes=32 * 2**20),
        name="table_rows",
    )(jnp.stack([lax.axis_index("dp"), lax.axis_index("wide")]), slot_of, wire, degrees[:, None], jnp.asarray(place, jnp.bfloat16))


def exchange(value, axis, count, bit):
    return lax.ppermute(value, axis, [(i, i ^ bit) for i in range(count)])


def wire_kernel(degrees, me_ref, forward_ref, inverse_ref, wire_ref, turned_ref):
    own, lat, order_count = forward_ref.shape
    owners, half, lanes = wire_ref.shape
    per_tile = 128 // lat
    me = me_ref[0]

    @pl.when(me < 2)
    def _():
        turned_ref[order_count:] = jnp.zeros((turned_ref.shape[0] - order_count, lanes), jnp.float32)
        turned_ref[:order_count, : own * lat] = forward_ref[...].reshape(own * lat, order_count).T
        if lanes > own * lat:
            turned_ref[:order_count, own * lat :] = jnp.zeros(
                (order_count, lanes - own * lat), jnp.float32
            )

    def forward_part(part):
        for owner in range(owners):
            first = owner * degrees + part * half
            wire_ref[owner] = turned_ref[first : first + half, :]

    def inverse_part(part):
        lane = lax.broadcasted_iota(jnp.int32, (half, 128), 1) // lat
        for owner in range(owners):
            first = owner * degrees + part * half
            rows = min(half, order_count - first)
            for tile in range(lanes // 128):
                value = jnp.zeros((rows, 128), jnp.float32)
                for place in range(per_tile):
                    slot = tile * per_tile + place
                    if slot < own:
                        found = inverse_ref[slot, first : first + rows, :]
                        found = jnp.concatenate([found] * per_tile, axis=1)
                        value = jnp.where(lane[:rows] == place, found, value)
                columns = slice(tile * 128, tile * 128 + 128)
                wire_ref[owner, :rows, columns] = value
                if rows < half:
                    wire_ref[owner, rows:, columns] = jnp.zeros((half - rows, 128), jnp.float32)

    pl.when(me == 0)(functools.partial(forward_part, 0))
    pl.when(me == 1)(functools.partial(forward_part, 1))
    pl.when(me == 2)(functools.partial(inverse_part, 0))
    pl.when(me == 3)(functools.partial(inverse_part, 1))


def tables_to_degrees(forward_table, inverse_table, wide_count, degree_slots, beside):
    own, lat_total, order_count = forward_table.shape
    dp_count = lax.axis_size("dp")
    half = -(-degree_slots // 16) * 8
    lanes = -(-own * lat_total // 128) * 128
    wire = pl.pallas_call(
        functools.partial(wire_kernel, degree_slots),
        in_specs=[pl.BlockSpec(memory_space=pltpu.SMEM)]
        + [pl.BlockSpec(memory_space=pltpu.VMEM)] * 2,
        out_specs=pl.BlockSpec(memory_space=pltpu.VMEM),
        out_shape=jax.ShapeDtypeStruct((wide_count, half, lanes), jnp.float32),
        scratch_shapes=[pltpu.VMEM((order_count + 2 * half - degree_slots + 8, lanes), jnp.float32)],
        compiler_params=pltpu.CompilerParams(vmem_limit_bytes=32 * 2**20),
        name="table_wire",
    )(lax.axis_index("dp")[None], forward_table, inverse_table)
    me = lax.axis_index("wide")
    pieces = [lax.dynamic_index_in_dim(wire, me ^ k, 0, keepdims=False) for k in range(wide_count)]
    pieces = [pieces[0]] + [exchange(pieces[k], "wide", wide_count, k) for k in range(1, wide_count)]
    wire, beside = lax.optimization_barrier((jnp.stack(pieces), beside))
    found = []
    for part, bits in ((wire[: wide_count // 2], (1, 2)), (wire[wide_count // 2 :], (2, 1))):
        by_index = {0: part}
        for bit in bits:
            names = list(by_index)
            passed = exchange(jnp.stack([by_index[i] for i in names]), "dp", dp_count, bit)
            by_index.update({i ^ bit: passed[k] for k, i in enumerate(names)})
        found.append(jnp.stack([by_index[i] for i in range(4)]))
    return jnp.concatenate(found, axis=1), beside


def reduce_halves(piece, bits):
    me = lax.axis_index("dp")
    for bit in bits:
        parts = piece.reshape((2, piece.shape[0] // 2) + piece.shape[1:])
        mine = (me & bit) // bit
        sent = lax.dynamic_index_in_dim(parts, 1 - mine, 0, keepdims=False)
        kept = lax.dynamic_index_in_dim(parts, mine, 0, keepdims=False)
        piece = kept + exchange(sent, "dp", 4, bit)
    return piece


def gather_half(piece, bit):
    other = exchange(piece, "dp", 4, bit)
    low = lax.axis_index("dp") & bit == 0
    return jnp.concatenate([jnp.where(low, piece, other), jnp.where(low, other, piece)], axis=0)


def gather_halves(piece, bits):
    for bit in bits[::-1]:
        piece = gather_half(piece, bit)
    return piece


def wide_sum(piece):
    wide_count = lax.axis_size("wide")
    bit = 1
    while bit < wide_count:
        piece = piece + exchange(piece, "wide", wide_count, bit)
        bit *= 2
    return piece


def by_bits():
    wide_count = lax.axis_size("wide")
    return lax.axis_size("dp") == 4 and wide_count & (wide_count - 1) == 0


def all_sum(rows):
    if not by_bits():
        return lax.psum(rows, ("dp", "wide"))
    return gather_halves(wide_sum(reduce_halves(rows, (1, 2))), (1, 2))


def thin_sum(thin, gram, cut):
    def squares(piece):
        product = jnp.einsum("cd,tdk->tck", gram, piece, precision=lax.Precision.HIGHEST)
        return jnp.sum(piece * product)

    me = lax.axis_index("dp")
    if not by_bits():
        thin = lax.psum(thin, "dp")
        parts = []
        for part in (thin[:cut], thin[cut:]):
            middle = part.shape[0] // 2
            parts.append((part[:middle], part[middle:], True))
        return parts, lax.psum(squares(thin), "wide")
    one, two = reduce_halves(thin[:cut], (1, 2)), reduce_halves(thin[cut:], (2, 1))
    total = jnp.broadcast_to(squares(one) + squares(two), (8, 128))
    for bit in (1, 2):
        total = total + exchange(total, "dp", 4, bit)
    total = wide_sum(total)[0, 0]
    one, two = gather_half(one, 2), gather_half(two, 1)
    parts = [
        (one, exchange(one, "dp", 4, 1), me & 1 == 0),
        (two, exchange(two, "dp", 4, 2), me & 2 == 0),
    ]
    return parts, total


def spectral_forward(spectra, fwd_rows, inv_rows, folded, lat_dev, fields):
    devices, order_count, lanes = spectra.shape
    lat_total = devices * lat_dev
    degrees, _, channels, width = folded.shape
    thin = 2 * channels
    slots = fwd_rows.shape[1]
    size = order_chunk(order_count, lat_total, width)
    groups = size // 8
    return pl.pallas_call(
        functools.partial(forward_kernel, lat_dev, fields),
        grid=(order_count // size,),
        in_specs=[
            pl.BlockSpec((devices, size, lanes), lambda i: (0, i, 0)),
            pl.BlockSpec((groups,) + fwd_rows.shape[1:], lambda i: (i, 0, 0)),
            pl.BlockSpec((groups,) + inv_rows.shape[1:], lambda i: (i, 0, 0)),
            pl.BlockSpec(folded.shape, lambda i: (0, 0, 0, 0)),
        ],
        out_specs=pl.BlockSpec((lat_total, size, 2 * width), lambda i: (0, i, 0)),
        out_shape=jax.ShapeDtypeStruct((lat_total, order_count, 2 * width), jnp.float32),
        scratch_shapes=[
            pltpu.VMEM((slots, size, thin), jnp.float32),
            pltpu.VMEM((slots, size, 2 * width), jnp.float32),
        ],
        compiler_params=vmem(60),
        name="spectral_forward",
    )(spectra, fwd_rows, inv_rows, folded)


def spectral_backward(grid_grad, spectra, fwd_rows, inv_rows, degrees, channels, fields):
    devices, order_count, lanes = spectra.shape
    lat_total = grid_grad.shape[0]
    lat_dev = lat_total // devices
    thin = 2 * channels
    block, first_steps, second_steps = adam_split(degrees)
    thin_slots = 2 * block * (first_steps + second_steps)
    width = grid_grad.shape[2] // 2
    slots = fwd_rows.shape[1]
    size = order_chunk(order_count, lat_total, width)
    groups = size // 8
    table = pl.BlockSpec((groups,) + fwd_rows.shape[1:], lambda i: (i, 0, 0))
    return pl.pallas_call(
        functools.partial(backward_kernel, degrees, lat_dev, fields),
        grid=(order_count // size,),
        in_specs=[
            pl.BlockSpec((lat_total, size, 2 * width), lambda i: (0, i, 0)),
            pl.BlockSpec((devices, size, lanes), lambda i: (0, i, 0)),
            table,
            table,
        ],
        out_specs=pl.BlockSpec((thin_slots, 2, channels, width), lambda i: (0, 0, 0, 0)),
        out_shape=jax.ShapeDtypeStruct((thin_slots, 2, channels, width), jnp.float32),
        scratch_shapes=[
            pltpu.VMEM((slots, size, thin), jnp.float32),
            pltpu.VMEM((slots, size, 2 * width), jnp.float32),
        ],
        compiler_params=vmem(60),
        name="spectral_backward",
    )(grid_grad, spectra, fwd_rows, inv_rows)


def adam_split(degrees):
    size = 3 if degrees % 3 == 0 and degrees >= 12 else 1
    steps_all = -(-degrees // (2 * size))
    return size, steps_all // 2, steps_all - steps_all // 2


def spectral_adam(factor, encoder, one, two, low_one, low_two, weights, done):
    weight = weights[0]
    degrees = weight.shape[0]
    size, first_steps, second_steps = adam_split(degrees)
    step = jnp.arange(first_steps + second_steps, dtype=jnp.int32)
    start_two = 2 * first_steps + jnp.where(low_two, 0, second_steps)
    block = jnp.where(
        step < first_steps, step + jnp.where(low_one, 0, first_steps), step - first_steps + start_two
    )
    block = jnp.minimum(block, degrees // size - 1)
    thin_block = jnp.where(step < first_steps, 0, block - start_two)
    whole = pl.BlockSpec((size,) + weight.shape[1:], lambda i, b, t: (b[i], 0, 0, 0))
    thin = (size,) + one.shape[1:]
    outs = [jax.ShapeDtypeStruct(weight.shape, jnp.float32)] * 3
    outs.append(jax.ShapeDtypeStruct(weight.shape, jnp.bfloat16))
    return pl.pallas_call(
        functools.partial(adam_kernel, first_steps),
        grid_spec=pltpu.PrefetchScalarGridSpec(
            num_scalar_prefetch=2,
            grid=(first_steps + second_steps,),
            in_specs=[
                pl.BlockSpec(memory_space=pltpu.SMEM),
                pl.BlockSpec(encoder.shape, lambda i, b, t: (0, 0)),
                pl.BlockSpec(thin, lambda i, b, t: (jnp.minimum(i, first_steps - 1), 0, 0, 0)),
                pl.BlockSpec(thin, lambda i, b, t: (t[i], 0, 0, 0)),
                whole,
                whole,
                whole,
            ]
            + [pl.BlockSpec(memory_space=pl.ANY)] * len(done),
            out_specs=[whole] * 4,
        ),
        out_shape=outs,
        input_output_aliases={9 + k: k for k in range(len(done))},
        compiler_params=vmem(48),
        name="spectral_adam",
    )(block, thin_block, factor, encoder, one, two, *weights, *done)


def pixel_weights(land_mask, missing_rows, first_row, lat_total, channels):
    lat_dev = land_mask.shape[0]
    latitude = (first_row + jnp.arange(lat_dev, dtype=jnp.int32)).astype(jnp.float32)
    cos_lat = jnp.sin(math.pi * (latitude + 0.5) / lat_total)
    sea_part = (1 - land_mask).astype(jnp.float32)
    valid_part = (1 - missing_rows).astype(jnp.float32) * cos_lat[:, None]
    sea_only = (jnp.arange(channels, dtype=jnp.int32) < SEA_CH)[:, None, None]
    return jnp.where(sea_only, sea_part[None], 1.0) * valid_part[None]


def adam_step(weight, moment_one, moment_two, gradient, decay_rate):
    first_new = BETA_ONE * moment_one + (1.0 - BETA_ONE) * gradient
    second_new = BETA_TWO * moment_two + (1.0 - BETA_TWO) * gradient * gradient
    first_hat = first_new * (1.0 / (1.0 - BETA_ONE**STEP))
    second_hat = second_new * (1.0 / (1.0 - BETA_TWO**STEP))
    weight_new = weight - LEARN_RATE * (
        first_hat / (jnp.sqrt(second_hat) + EPSILON) + decay_rate * weight
    )
    return (weight_new, first_new, second_new)


def body(
    inputs,
    targets,
    land_mask,
    missing_mask,
    order_map,
    degree_map,
    forward_table,
    inverse_table,
    spectral_weight,
    spectral_first,
    spectral_second,
    io_weight,
    io_first,
    io_second,
    mlp_weight,
    mlp_first,
    mlp_second,
    biases,
    bias_first,
    bias_second,
):
    fields = inputs[0]
    truth = targets[0]
    lat_dev = fields.shape[1]
    lon_count = fields.shape[2]
    channels = io_weight.shape[1]
    width = io_weight.shape[2]
    hidden_units = mlp_weight.shape[2]
    wide_count = lax.axis_size("wide")
    position = lax.axis_index("wide")
    order_count = order_map.shape[0]
    degree_slots = spectral_weight.shape[0]
    lat_total = lat_dev * wide_count
    entries = lax.axis_size("dp") * channels * lat_total * lon_count
    forward, inverse = dft_tables(order_count, lon_count)

    enc_bias = biases[:width]
    hidden_bias = biases[width : width + hidden_units]
    mlp_bias = biases[width + hidden_units : 2 * width + hidden_units]
    out_bias = biases[2 * width + hidden_units :]
    thin_count = -(-(channels + 1) // 16) * 16
    spare = thin_count - channels - 1
    encoder = jnp.concatenate(
        [io_weight[0], enc_bias[None], jnp.zeros((spare, width), jnp.float32)], axis=0
    )

    lines = fields.transpose(1, 0, 2).reshape(lat_dev * channels, lon_count)
    spectra = [dot("rj,sj->sr", lines, table) for table in forward]
    spare = -2 * lat_dev * channels % 128
    spectra = jnp.concatenate(spectra + [jnp.zeros((order_count, spare), jnp.float32)], axis=1)

    folded = dot("cd,tpdk->tpck", encoder, spectral_weight)

    my_degrees = lax.dynamic_slice_in_dim(degree_map, position * degree_slots, degree_slots)
    slot_of = jnp.argsort(order_map)
    slots = degree_slots + degree_slots % 2
    if 128 % lat_total == 0 and lax.axis_size("dp") == 4 and wide_count == 8 and lat_total >= 8:
        wire, (folded, spectra) = tables_to_degrees(
            forward_table, inverse_table, wide_count, degree_slots, (folded, spectra)
        )
        degrees = jnp.pad(my_degrees, (0, 2 * wire.shape[2] - degree_slots), constant_values=-1)
        own = forward_table.shape[0]
        fwd_rows, inv_rows = table_rows(wire, slot_of, degrees, own, lat_total, slots)
    else:
        fwd_table = lax.all_to_all(forward_table, "wide", split_axis=2, concat_axis=0, tiled=True)
        inv_table = lax.all_to_all(inverse_table, "wide", split_axis=1, concat_axis=0, tiled=True)
        orders = jnp.arange(order_count, dtype=jnp.int32)
        live = (
            (my_degrees[None, :] >= orders[:, None])
            & (orders[:, None] < M)
            & (my_degrees[None, :] < L)
        ).astype(jnp.float32)
        even = ((0, 0), (0, degree_slots % 2), (0, 0), (0, 0))
        fwd_masked = fwd_table[slot_of] * live[:, None, :]
        inv_masked = inv_table[slot_of] * live[:, :, None]
        fwd_masked = fwd_masked.reshape(order_count // 8, 8, lat_total, degree_slots)
        inv_masked = inv_masked.reshape(order_count // 8, 8, degree_slots, lat_total)

        def by_degree(table):
            return jnp.pad(table, even).reshape(order_count // 8, slots, lat_total * 8)

        fwd_rows = by_degree(fwd_masked.transpose(0, 3, 2, 1))
        inv_rows = by_degree(inv_masked.transpose(0, 2, 3, 1))

    spectra = lax.all_gather(spectra, "wide", axis=0, tiled=False)
    grid_coef = spectral_forward(spectra, fwd_rows, inv_rows, folded, lat_dev, channels)
    grid_coef = lax.psum_scatter(grid_coef, "wide", scatter_dimension=0, tiled=True)
    grid_coef = grid_coef.reshape(lat_dev, order_count, 2, width)

    encoded = dot("caj,ck->ajk", fields, io_weight[0]) + enc_bias
    mixed_in = encoded + dot("aspc,psj->ajc", grid_coef, inverse)
    hidden_pre = dot("ajk,kh->ajh", mixed_in, mlp_weight[0]) + hidden_bias
    hidden_act, smooth_back = jax.vjp(smooth, hidden_pre)
    latent = mixed_in + dot("ajh,kh->ajk", hidden_act, mlp_weight[1]) + mlp_bias
    predicted = dot("ajk,ck->caj", latent, io_weight[1]) + out_bias[:, None, None]
    misfit = predicted - truth
    pixel_weight = pixel_weights(land_mask, missing_mask[0], position * lat_dev, lat_total, channels)
    count_local = jnp.sum(pixel_weight)
    weighted = pixel_weight * misfit
    loss_local = jnp.sum(weighted * misfit)
    pred_grad = weighted * (2.0 / entries)
    out_bias_grad = jnp.sum(pred_grad, axis=(1, 2))
    decoder_grad = dot("caj,ajk->ck", pred_grad, latent)
    latent_grad = dot("caj,ck->ajk", pred_grad, io_weight[1])
    mlp_bias_grad = jnp.sum(latent_grad, axis=(0, 1))
    down_grad = dot("ajk,ajh->kh", latent_grad, hidden_act)
    act_grad = dot("ajk,kh->ajh", latent_grad, mlp_weight[1])
    pre_grad = smooth_back(act_grad)[0]
    hidden_bias_grad = jnp.sum(pre_grad, axis=(0, 1))
    up_grad = dot("ajk,ajh->kh", mixed_in, pre_grad)
    mixed_grad = latent_grad + dot("ajh,kh->ajk", pre_grad, mlp_weight[0])

    grid_grad = dot("ajc,psj->aspc", mixed_grad, inverse).reshape(lat_dev, order_count, 2 * width)
    grid_grad = lax.all_gather(grid_grad, "wide", axis=0, tiled=True)
    direct = dot("caj,ajk->ck", fields, mixed_grad)
    direct_bias = jnp.sum(mixed_grad, axis=(0, 1))
    small = [direct_bias, hidden_bias_grad, mlp_bias_grad, out_bias_grad, loss_local[None], count_local[None]]
    small = jnp.concatenate(small)
    small_count = small.shape[0]
    flat = [up_grad.reshape(-1, width), down_grad.reshape(-1, width), decoder_grad, direct]
    flat.append(jnp.pad(small, (0, -small_count % width)).reshape(-1, width))
    flat = jnp.concatenate(flat, axis=0)
    flat = all_sum(jnp.pad(flat, ((0, -flat.shape[0] % 32), (0, 0))))
    grid_grad, flat = lax.optimization_barrier((grid_grad, flat))
    thin = spectral_backward(
        grid_grad, spectra, fwd_rows, inv_rows, degree_slots, thin_count, channels
    )
    at = 2 * hidden_units
    mlp_grad = flat[:at].reshape(2, width, hidden_units)
    decoder_grad = flat[at : at + channels]
    direct = flat[at + channels : at + 2 * channels]
    small = flat[at + 2 * channels :].reshape(-1)[:small_count]
    encoder_grad = all_sum(dot("tpck,tpdk->cd", thin[:degree_slots], spectral_weight))
    gram = jnp.einsum("ck,dk->cd", encoder, encoder, precision=lax.Precision.HIGHEST)
    size, first_steps, _ = adam_split(degree_slots)
    pairs = thin.reshape((-1,) + thin.shape[2:])
    parts, spectral_squares = thin_sum(pairs, gram, 4 * size * first_steps)
    io_grad = jnp.stack([direct + encoder_grad[:channels], decoder_grad])
    bias_grad = jnp.concatenate([small[:width] + encoder_grad[channels], small[width:-2]])
    loss_sum, valid_weight = small[-2], small[-1]
    rescale = entries / valid_weight
    squares = (
        spectral_squares
        + jnp.sum(io_grad * io_grad)
        + jnp.sum(mlp_grad * mlp_grad)
        + jnp.sum(bias_grad * bias_grad)
    )
    grad_norm = jnp.sqrt(squares) * rescale
    factor = rescale * CLIP_LIMIT / jnp.maximum(grad_norm, CLIP_LIMIT)
    spectral = ()
    weights = (spectral_weight, spectral_first, spectral_second)
    for half in range(2):
        one, two = (part[half].reshape((-1, 2) + thin.shape[2:]) for part in parts)
        low_one, low_two = ((part[2] if half == 0 else jnp.logical_not(part[2])) for part in parts)
        spectral = spectral_adam(factor[None], encoder, one, two, low_one, low_two, weights, spectral)
    spectral_new, spectral_first_new, spectral_second_new, spectral_low = spectral
    io_new, io_first_new, io_second_new = adam_step(
        io_weight, io_first, io_second, io_grad * factor, WEIGHT_DECAY
    )
    mlp_new, mlp_first_new, mlp_second_new = adam_step(
        mlp_weight, mlp_first, mlp_second, mlp_grad * factor, WEIGHT_DECAY
    )
    bias_new, bias_first_new, bias_second_new = adam_step(
        biases, bias_first, bias_second, bias_grad * factor, 0.0
    )
    return (
        loss_sum,
        valid_weight,
        grad_norm,
        spectral_new,
        spectral_first_new,
        spectral_second_new,
        spectral_low,
        io_new,
        io_first_new,
        io_second_new,
        io_new.astype(jnp.bfloat16),
        mlp_new,
        mlp_first_new,
        mlp_second_new,
        mlp_new.astype(jnp.bfloat16),
        bias_new,
        bias_first_new,
        bias_second_new,
        bias_new.astype(jnp.bfloat16),
    )


def solution(mesh):
    wide4 = P("wide", None, None, None)
    in_specs = (
        P("dp", None, "wide", None),
        P("dp", None, "wide", None),
        P("wide", None),
        P("dp", "wide", None),
        P(),
        P(),
        P("wide", None, None),
        P("wide", None, None),
        wide4,
        wide4,
        wide4,
    ) + (P(),) * 9
    out_specs = (P(),) * 3 + (wide4,) * 4 + (P(),) * 12
    return jax.shard_map(body, mesh=mesh, in_specs=in_specs, out_specs=out_specs, check_vma=False)
```

```python
import functools
import math

import jax
import jax.numpy as jnp
import numpy as np
from jax import lax
from jax.experimental import pallas as pl
from jax.experimental.pallas import tpu as pltpu
from jax.sharding import PartitionSpec as P

M = 360
L = 360
SEA_CH = 1
STEP = 5


HIGH = lax.Precision.HIGH
CLIP_LIMIT = 0.001
LEARN_RATE = 0.1
BETA_ONE = 0.9
BETA_TWO = 0.999
EPSILON = 1e-08
WEIGHT_DECAY = 0.1


def smooth(values):
    return jax.nn.gelu(values, approximate=True)


def dot(spec, left, right):
    return jnp.einsum(spec, left, right, precision=HIGH)


def dft_tables(order_count, lon_count):
    orders = np.arange(order_count, dtype=np.int64)[:, None]
    columns = np.arange(lon_count, dtype=np.int64)[None, :]
    angle = (orders * columns % lon_count) * (2.0 * math.pi / lon_count)
    both = np.stack([np.cos(angle), -np.sin(angle)], axis=0)
    factor = np.where(orders == 0, 1.0, 2.0)[None]
    return (both / lon_count).astype(np.float32), (factor * both).astype(np.float32)


def halves(value):
    high = value.astype(jnp.bfloat16)
    low = (value - high.astype(jnp.float32)).astype(jnp.bfloat16)
    return high, low


def dot3(left, right, dims=(((1,), (0,)), ((), ()))):
    left_high, left_low = halves(left)
    right_high, right_low = halves(right)

    def one(a, b):
        return lax.dot_general(a, b, dims, preferred_element_type=jnp.float32)

    return one(left_high, right_high) + (one(left_high, right_low) + one(left_low, right_high))


def block_diagonal(rows):
    count, lanes = rows.shape
    spread = jnp.broadcast_to(rows[:, None, :], (count, 8, lanes))
    sub = lax.broadcasted_iota(jnp.int32, (count, 8, lanes), 1)
    lane = lax.broadcasted_iota(jnp.int32, (count, 8, lanes), 2) & 7
    return jnp.where(sub == lane, spread, 0.0).reshape(count * 8, lanes)


def steps(count):
    return max(size for size in range(1, 16) if count % size == 0)


def group_rows(group):
    return pl.ds(pl.multiple_of(group * 8, 8), 8)


def legendre(values, table, out_ref, group):
    lat, _, lanes = values.shape
    product = dot3(block_diagonal(table), values.reshape(lat * 8, lanes))
    out_ref[:, group_rows(group), :] = product.reshape(product.shape[0] // 8, 8, lanes)


def channel_spectra(spec_ref, lat_dev, channels, thin, group):
    devices, size, lanes = spec_ref.shape
    spectra = spec_ref[:, group_rows(group), :].reshape(devices * 8, lanes)
    lane = lax.broadcasted_iota(jnp.int32, (devices * 8, lanes), 1)
    order = lax.broadcasted_iota(jnp.int32, (devices * 8, lanes), 0) & 7
    order += pl.program_id(0) * size + group * 8
    ones = jnp.where((order == 0) & (lane == channels), 1.0, 0.0)
    half = thin // 2
    rows = []
    for row in range(lat_dev):
        real = row * channels
        imag = (lat_dev + row) * channels
        left = pltpu.roll(spectra, (lanes - real) % lanes, 1) if row else spectra
        right = pltpu.roll(spectra, (half - imag) % lanes, 1)
        value = jnp.where((lane >= half) & (lane < half + channels), right, ones)
        value = jnp.where(lane < channels, left, value)
        rows.append(value[:, :thin].reshape(devices, 8, thin))
    return jnp.stack(rows, axis=1).reshape(devices * lat_dev, 8, thin)


def forward_kernel(lat_dev, channels, spec_ref, fwd_ref, inv_ref, folded_ref, grid_ref, coef_ref, mixed_ref):
    groups = fwd_ref.shape[0]
    degrees = folded_ref.shape[0]
    slots = mixed_ref.shape[0]
    for spare in range(degrees, slots):
        mixed_ref[spare] = jnp.zeros(mixed_ref.shape[1:], jnp.float32)

    thin = coef_ref.shape[2]

    def analyse(group, carry):
        spectra = channel_spectra(spec_ref, lat_dev, channels, thin, group)
        legendre(spectra, fwd_ref[group], coef_ref, group)
        return carry

    lax.fori_loop(0, groups, analyse, 0, unroll=steps(groups))

    def mix(degree, carry):
        real = folded_ref[degree, 0]
        imag = folded_ref[degree, 1]
        block = jnp.concatenate(
            [jnp.concatenate([real, imag], axis=1), jnp.concatenate([-imag, real], axis=1)], axis=0
        )
        mixed_ref[degree] = dot3(coef_ref[degree], block)
        return carry

    lax.fori_loop(0, degrees, mix, 0, unroll=steps(degrees))

    def synthesise(group, carry):
        rows = pl.ds(pl.multiple_of(group * 8, 8), 8)
        mixed = mixed_ref[:, rows, :]
        product = dot3(
            block_diagonal(inv_ref[group]),
            mixed.reshape(slots * 8, mixed.shape[2]),
            (((0,), (0,)), ((), ())),
        )
        grid_ref[:, rows, :] = product.reshape(product.shape[0] // 8, 8, mixed.shape[2])
        return carry

    lax.fori_loop(0, groups, synthesise, 0, unroll=steps(groups))


def backward_kernel(degrees, lat_dev, fields, grid_ref, spec_ref, fwd_ref, inv_ref, thin_ref, coef_ref, out_ref):
    groups = fwd_ref.shape[0]
    _, _, channels, width = thin_ref.shape

    @pl.when(pl.program_id(0) == 0)
    def _():
        thin_ref[...] = jnp.zeros(thin_ref.shape, jnp.float32)

    def analyse(group, carry):
        spectra = channel_spectra(spec_ref, lat_dev, fields, 2 * channels, group)
        legendre(spectra, fwd_ref[group], coef_ref, group)
        legendre(grid_ref[:, group_rows(group), :], inv_ref[group], out_ref, group)
        return carry

    lax.fori_loop(0, groups, analyse, 0, unroll=steps(groups))

    def product(degree, carry):
        both = dot3(coef_ref[degree], out_ref[degree], (((0,), (0,)), ((), ())))
        thin_ref[degree, 0] += both[:channels, :width] + both[channels:, width:]
        thin_ref[degree, 1] += both[:channels, width:] - both[channels:, :width]
        return carry

    lax.fori_loop(0, degrees, product, 0, unroll=steps(degrees))


def adam_kernel(first_steps, block_ref, thin_block_ref, factor_ref, encoder_ref, *refs):
    one_ref, two_ref, weight_ref, first_ref, second_ref = refs[:5]
    weight_out, first_out, second_out, low_out = refs[-4:]
    factor = factor_ref[0]
    in_one = pl.program_id(0) < first_steps
    encoder_high, encoder_low = halves(encoder_ref[...])
    left = jnp.concatenate([encoder_high, encoder_high, encoder_low], axis=0)
    for degree, part in np.ndindex(one_ref.shape[:2]):
        thin = jnp.where(in_one, one_ref[degree, part], two_ref[degree, part])
        high, low = halves(thin * factor)
        right = jnp.concatenate([high, low, high], axis=0)
        gradient = lax.dot_general(
            left, right, (((0,), (0,)), ((), ())), preferred_element_type=jnp.float32
        )
        weight, first, second = adam_step(
            weight_ref[degree, part], first_ref[degree, part], second_ref[degree, part], gradient, WEIGHT_DECAY
        )
        weight_out[degree, part] = weight
        first_out[degree, part] = first
        second_out[degree, part] = second
        low_out[degree, part] = weight.astype(jnp.bfloat16)


def table_kernel(own, me_ref, slot_ref, wire_ref, degree_ref, place_ref, *rows_refs):
    groups, slots, lanes = rows_refs[0].shape
    lat = lanes // 8
    per_tile = 128 // lat
    degree = degree_ref[...]
    count = degree.shape[0]
    lane = lax.broadcasted_iota(jnp.int32, (count, 128), 1) // lat
    me = me_ref[0]
    me_wide = me_ref[1]

    def one_group(group, carry):
        found = ([], [])
        for first in range(0, 8, per_tile):
            tiles = [jnp.zeros((count, 128), jnp.float32)] * 2
            for place in range(per_tile):
                order = group * 8 + first + place
                slot = slot_ref[order]
                source = slot // own
                at = slot - source * own
                block = at // per_tile
                columns = pl.ds(pl.multiple_of(block * 128, 128), 128)
                shift = lax.rem((place - (at - block * per_tile)) * lat + 128, 128)
                live = (degree >= order) & (order < M) & (degree < L) & (lane == place)
                for table in range(2):
                    both = [wire_ref[(2 * table + half) ^ me, source ^ me_wide, :, columns] for half in range(2)]
                    moved = pltpu.roll(jnp.concatenate(both, axis=0), shift, 1)
                    tiles[table] = jnp.where(live, moved, tiles[table])
            for table in range(2):
                found[table].append(tiles[table])
        place = place_ref[...]
        for table in range(2):
            high, low = halves(jnp.concatenate(found[table], axis=1))
            rows = jnp.dot(high, place, preferred_element_type=jnp.float32)
            rows += jnp.dot(low, place, preferred_element_type=jnp.float32)
            rows_refs[table][group] = rows[:slots]
        return carry

    lax.fori_loop(0, groups, one_group, 0, unroll=steps(groups))


def order_chunk(order_count, lat_total, width):
    best = 8
    for size in range(8, order_count + 1, 8):
        if order_count % size == 0 and lat_total * size * width * 8 <= 8.5 * 2**20:
            best = size
    return best


def vmem(mebibytes):
    return pltpu.CompilerParams(
        dimension_semantics=("arbitrary",), vmem_limit_bytes=mebibytes * 2**20
    )


def table_rows(wire, slot_of, degrees, own, lat_total, slots):
    groups = slot_of.shape[0] // 8
    lane = np.arange(lat_total * 8)
    place = np.zeros((lat_total * 8, lat_total * 8), np.float32)
    place[lane, lane % lat_total * 8 + lane // lat_total] = 1.0
    return pl.pallas_call(
        functools.partial(table_kernel, own),
        in_specs=[pl.BlockSpec(memory_space=pltpu.SMEM)] * 2
        + [pl.BlockSpec(memory_space=pltpu.VMEM)] * 3,
        out_specs=[pl.BlockSpec(memory_space=pltpu.VMEM)] * 2,
        out_shape=[jax.ShapeDtypeStruct((groups, slots, lat_total * 8), jnp.float32)] * 2,
        compiler_params=pltpu.CompilerParams(vmem_limit_bytes=32 * 2**20),
        name="table_rows",
    )(jnp.stack([lax.axis_index("dp"), lax.axis_index("wide")]), slot_of, wire, degrees[:, None], jnp.asarray(place, jnp.bfloat16))


def exchange(value, axis, count, bit):
    return lax.ppermute(value, axis, [(i, i ^ bit) for i in range(count)])


def wire_kernel(degrees, me_ref, forward_ref, inverse_ref, wire_ref, turned_ref):
    own, lat, order_count = forward_ref.shape
    owners, half, lanes = wire_ref.shape
    me = me_ref[0]

    def turn(table_ref):
        turned_ref[order_count:] = jnp.zeros((turned_ref.shape[0] - order_count, lanes), jnp.float32)
        turned_ref[:order_count, : own * lat] = table_ref[...].reshape(own * lat, order_count).T
        if lanes > own * lat:
            turned_ref[:order_count, own * lat :] = jnp.zeros(
                (order_count, lanes - own * lat), jnp.float32
            )

    def hand_out(part):
        for owner in range(owners):
            first = owner * degrees + part * half
            wire_ref[owner] = turned_ref[first : first + half, :]

    pl.when(me < 2)(functools.partial(turn, forward_ref))
    pl.when(me >= 2)(functools.partial(turn, inverse_ref))
    pl.when(me % 2 == 0)(functools.partial(hand_out, 0))
    pl.when(me % 2 == 1)(functools.partial(hand_out, 1))


def tables_to_degrees(forward_table, inverse_table, wide_count, degree_slots, beside):
    own, lat_total, order_count = forward_table.shape
    dp_count = lax.axis_size("dp")
    half = -(-degree_slots // 16) * 8
    lanes = -(-own * lat_total // 128) * 128
    wire = pl.pallas_call(
        functools.partial(wire_kernel, degree_slots),
        in_specs=[pl.BlockSpec(memory_space=pltpu.SMEM)]
        + [pl.BlockSpec(memory_space=pltpu.VMEM)] * 2,
        out_specs=pl.BlockSpec(memory_space=pltpu.VMEM),
        out_shape=jax.ShapeDtypeStruct((wide_count, half, lanes), jnp.float32),
        scratch_shapes=[pltpu.VMEM((order_count + 2 * half - degree_slots + 8, lanes), jnp.float32)],
        compiler_params=pltpu.CompilerParams(vmem_limit_bytes=32 * 2**20),
        name="table_wire",
    )(lax.axis_index("dp")[None], forward_table, inverse_table.transpose(0, 2, 1))
    me = lax.axis_index("wide")
    pieces = [lax.dynamic_index_in_dim(wire, me ^ k, 0, keepdims=False) for k in range(wide_count)]
    pieces = [pieces[0]] + [exchange(pieces[k], "wide", wide_count, k) for k in range(1, wide_count)]
    wire, beside = lax.optimization_barrier((jnp.stack(pieces), beside))
    found = []
    for part, bits in ((wire[: wide_count // 2], (1, 2)), (wire[wide_count // 2 :], (2, 1))):
        by_index = {0: part}
        for bit in bits:
            names = list(by_index)
            passed = exchange(jnp.stack([by_index[i] for i in names]), "dp", dp_count, bit)
            by_index.update({i ^ bit: passed[k] for k, i in enumerate(names)})
        found.append(jnp.stack([by_index[i] for i in range(4)]))
    return jnp.concatenate(found, axis=1), beside


def reduce_halves(piece, bits):
    me = lax.axis_index("dp")
    for bit in bits:
        parts = piece.reshape((2, piece.shape[0] // 2) + piece.shape[1:])
        mine = (me & bit) // bit
        sent = lax.dynamic_index_in_dim(parts, 1 - mine, 0, keepdims=False)
        kept = lax.dynamic_index_in_dim(parts, mine, 0, keepdims=False)
        piece = kept + exchange(sent, "dp", 4, bit)
    return piece


def gather_half(piece, bit):
    other = exchange(piece, "dp", 4, bit)
    low = lax.axis_index("dp") & bit == 0
    return jnp.concatenate([jnp.where(low, piece, other), jnp.where(low, other, piece)], axis=0)


def gather_halves(piece, bits):
    for bit in bits[::-1]:
        piece = gather_half(piece, bit)
    return piece


def wide_sum(piece):
    wide_count = lax.axis_size("wide")
    bit = 1
    while bit < wide_count:
        piece = piece + exchange(piece, "wide", wide_count, bit)
        bit *= 2
    return piece


def by_bits():
    wide_count = lax.axis_size("wide")
    return lax.axis_size("dp") == 4 and wide_count & (wide_count - 1) == 0


def all_sum(rows):
    if not by_bits():
        return lax.psum(rows, ("dp", "wide"))
    return gather_halves(wide_sum(reduce_halves(rows, (1, 2))), (1, 2))


def thin_sum(thin, gram, cut):
    def squares(piece):
        product = jnp.einsum("cd,tdk->tck", gram, piece, precision=lax.Precision.HIGHEST)
        return jnp.sum(piece * product)

    me = lax.axis_index("dp")
    if not by_bits():
        thin = lax.psum(thin, "dp")
        parts = []
        for part in (thin[:cut], thin[cut:]):
            middle = part.shape[0] // 2
            parts.append((part[:middle], part[middle:], True))
        return parts, lax.psum(squares(thin), "wide")
    one, two = reduce_halves(thin[:cut], (1, 2)), reduce_halves(thin[cut:], (2, 1))
    total = jnp.broadcast_to(squares(one) + squares(two), (8, 128))
    for bit in (1, 2):
        total = total + exchange(total, "dp", 4, bit)
    total = wide_sum(total)[0, 0]
    one, two = gather_half(one, 2), gather_half(two, 1)
    parts = [
        (one, exchange(one, "dp", 4, 1), me & 1 == 0),
        (two, exchange(two, "dp", 4, 2), me & 2 == 0),
    ]
    return parts, total


def spectral_forward(spectra, fwd_rows, inv_rows, folded, lat_dev, fields):
    devices, order_count, lanes = spectra.shape
    lat_total = devices * lat_dev
    degrees, _, channels, width = folded.shape
    thin = 2 * channels
    slots = fwd_rows.shape[1]
    size = order_chunk(order_count, lat_total, width)
    groups = size // 8
    return pl.pallas_call(
        functools.partial(forward_kernel, lat_dev, fields),
        grid=(order_count // size,),
        in_specs=[
            pl.BlockSpec((devices, size, lanes), lambda i: (0, i, 0)),
            pl.BlockSpec((groups,) + fwd_rows.shape[1:], lambda i: (i, 0, 0)),
            pl.BlockSpec((groups,) + inv_rows.shape[1:], lambda i: (i, 0, 0)),
            pl.BlockSpec(folded.shape, lambda i: (0, 0, 0, 0)),
        ],
        out_specs=pl.BlockSpec((lat_total, size, 2 * width), lambda i: (0, i, 0)),
        out_shape=jax.ShapeDtypeStruct((lat_total, order_count, 2 * width), jnp.float32),
        scratch_shapes=[
            pltpu.VMEM((slots, size, thin), jnp.float32),
            pltpu.VMEM((slots, size, 2 * width), jnp.float32),
        ],
        compiler_params=vmem(60),
        name="spectral_forward",
    )(spectra, fwd_rows, inv_rows, folded)


def spectral_backward(grid_grad, spectra, fwd_rows, inv_rows, degrees, channels, fields):
    devices, order_count, lanes = spectra.shape
    lat_total = grid_grad.shape[0]
    lat_dev = lat_total // devices
    thin = 2 * channels
    block, first_steps, second_steps = adam_split(degrees)
    thin_slots = 2 * block * (first_steps + second_steps)
    width = grid_grad.shape[2] // 2
    slots = fwd_rows.shape[1]
    size = order_chunk(order_count, lat_total, width)
    groups = size // 8
    table = pl.BlockSpec((groups,) + fwd_rows.shape[1:], lambda i: (i, 0, 0))
    return pl.pallas_call(
        functools.partial(backward_kernel, degrees, lat_dev, fields),
        grid=(order_count // size,),
        in_specs=[
            pl.BlockSpec((lat_total, size, 2 * width), lambda i: (0, i, 0)),
            pl.BlockSpec((devices, size, lanes), lambda i: (0, i, 0)),
            table,
            table,
        ],
        out_specs=pl.BlockSpec((thin_slots, 2, channels, width), lambda i: (0, 0, 0, 0)),
        out_shape=jax.ShapeDtypeStruct((thin_slots, 2, channels, width), jnp.float32),
        scratch_shapes=[
            pltpu.VMEM((slots, size, thin), jnp.float32),
            pltpu.VMEM((slots, size, 2 * width), jnp.float32),
        ],
        compiler_params=vmem(60),
        name="spectral_backward",
    )(grid_grad, spectra, fwd_rows, inv_rows)


def adam_split(degrees):
    size = 3 if degrees % 3 == 0 and degrees >= 12 else 1
    steps_all = -(-degrees // (2 * size))
    return size, steps_all // 2, steps_all - steps_all // 2


def spectral_adam(factor, encoder, one, two, low_one, low_two, weights, done):
    weight = weights[0]
    degrees = weight.shape[0]
    size, first_steps, second_steps = adam_split(degrees)
    step = jnp.arange(first_steps + second_steps, dtype=jnp.int32)
    start_two = 2 * first_steps + jnp.where(low_two, 0, second_steps)
    block = jnp.where(
        step < first_steps, step + jnp.where(low_one, 0, first_steps), step - first_steps + start_two
    )
    block = jnp.minimum(block, degrees // size - 1)
    thin_block = jnp.where(step < first_steps, 0, block - start_two)
    whole = pl.BlockSpec((size,) + weight.shape[1:], lambda i, b, t: (b[i], 0, 0, 0))
    thin = (size,) + one.shape[1:]
    outs = [jax.ShapeDtypeStruct(weight.shape, jnp.float32)] * 3
    outs.append(jax.ShapeDtypeStruct(weight.shape, jnp.bfloat16))
    return pl.pallas_call(
        functools.partial(adam_kernel, first_steps),
        grid_spec=pltpu.PrefetchScalarGridSpec(
            num_scalar_prefetch=2,
            grid=(first_steps + second_steps,),
            in_specs=[
                pl.BlockSpec(memory_space=pltpu.SMEM),
                pl.BlockSpec(encoder.shape, lambda i, b, t: (0, 0)),
                pl.BlockSpec(thin, lambda i, b, t: (jnp.minimum(i, first_steps - 1), 0, 0, 0)),
                pl.BlockSpec(thin, lambda i, b, t: (t[i], 0, 0, 0)),
                whole,
                whole,
                whole,
            ]
            + [pl.BlockSpec(memory_space=pl.ANY)] * len(done),
            out_specs=[whole] * 4,
        ),
        out_shape=outs,
        input_output_aliases={9 + k: k for k in range(len(done))},
        compiler_params=vmem(48),
        name="spectral_adam",
    )(block, thin_block, factor, encoder, one, two, *weights, *done)


def pixel_weights(land_mask, missing_rows, first_row, lat_total, channels):
    lat_dev = land_mask.shape[0]
    latitude = (first_row + jnp.arange(lat_dev, dtype=jnp.int32)).astype(jnp.float32)
    cos_lat = jnp.sin(math.pi * (latitude + 0.5) / lat_total)
    sea_part = (1 - land_mask).astype(jnp.float32)
    valid_part = (1 - missing_rows).astype(jnp.float32) * cos_lat[:, None]
    sea_only = (jnp.arange(channels, dtype=jnp.int32) < SEA_CH)[:, None, None]
    return jnp.where(sea_only, sea_part[None], 1.0) * valid_part[None]


def adam_step(weight, moment_one, moment_two, gradient, decay_rate):
    first_new = BETA_ONE * moment_one + (1.0 - BETA_ONE) * gradient
    second_new = BETA_TWO * moment_two + (1.0 - BETA_TWO) * gradient * gradient
    first_hat = first_new * (1.0 / (1.0 - BETA_ONE**STEP))
    second_hat = second_new * (1.0 / (1.0 - BETA_TWO**STEP))
    weight_new = weight - LEARN_RATE * (
        first_hat / (jnp.sqrt(second_hat) + EPSILON) + decay_rate * weight
    )
    return (weight_new, first_new, second_new)


def body(
    inputs,
    targets,
    land_mask,
    missing_mask,
    order_map,
    degree_map,
    forward_table,
    inverse_table,
    spectral_weight,
    spectral_first,
    spectral_second,
    io_weight,
    io_first,
    io_second,
    mlp_weight,
    mlp_first,
    mlp_second,
    biases,
    bias_first,
    bias_second,
):
    fields = inputs[0]
    truth = targets[0]
    lat_dev = fields.shape[1]
    lon_count = fields.shape[2]
    channels = io_weight.shape[1]
    width = io_weight.shape[2]
    hidden_units = mlp_weight.shape[2]
    wide_count = lax.axis_size("wide")
    position = lax.axis_index("wide")
    order_count = order_map.shape[0]
    degree_slots = spectral_weight.shape[0]
    lat_total = lat_dev * wide_count
    entries = lax.axis_size("dp") * channels * lat_total * lon_count
    forward, inverse = dft_tables(order_count, lon_count)

    enc_bias = biases[:width]
    hidden_bias = biases[width : width + hidden_units]
    mlp_bias = biases[width + hidden_units : 2 * width + hidden_units]
    out_bias = biases[2 * width + hidden_units :]
    thin_count = -(-(channels + 1) // 16) * 16
    spare = thin_count - channels - 1
    encoder = jnp.concatenate(
        [io_weight[0], enc_bias[None], jnp.zeros((spare, width), jnp.float32)], axis=0
    )

    lines = fields.transpose(1, 0, 2).reshape(lat_dev * channels, lon_count)
    spectra = [dot("rj,sj->sr", lines, table) for table in forward]
    spare = -2 * lat_dev * channels % 128
    spectra = jnp.concatenate(spectra + [jnp.zeros((order_count, spare), jnp.float32)], axis=1)

    folded = dot("cd,tpdk->tpck", encoder, spectral_weight)

    my_degrees = lax.dynamic_slice_in_dim(degree_map, position * degree_slots, degree_slots)
    slot_of = jnp.argsort(order_map)
    slots = degree_slots + degree_slots % 2
    if 128 % lat_total == 0 and lax.axis_size("dp") == 4 and wide_count == 8 and lat_total >= 8:
        wire, (folded, spectra) = tables_to_degrees(
            forward_table, inverse_table, wide_count, degree_slots, (folded, spectra)
        )
        degrees = jnp.pad(my_degrees, (0, 2 * wire.shape[2] - degree_slots), constant_values=-1)
        own = forward_table.shape[0]
        fwd_rows, inv_rows = table_rows(wire, slot_of, degrees, own, lat_total, slots)
    else:
        fwd_table = lax.all_to_all(forward_table, "wide", split_axis=2, concat_axis=0, tiled=True)
        inv_table = lax.all_to_all(inverse_table, "wide", split_axis=1, concat_axis=0, tiled=True)
        orders = jnp.arange(order_count, dtype=jnp.int32)
        live = (
            (my_degrees[None, :] >= orders[:, None])
            & (orders[:, None] < M)
            & (my_degrees[None, :] < L)
        ).astype(jnp.float32)
        even = ((0, 0), (0, degree_slots % 2), (0, 0), (0, 0))
        fwd_masked = fwd_table[slot_of] * live[:, None, :]
        inv_masked = inv_table[slot_of] * live[:, :, None]
        fwd_masked = fwd_masked.reshape(order_count // 8, 8, lat_total, degree_slots)
        inv_masked = inv_masked.reshape(order_count // 8, 8, degree_slots, lat_total)

        def by_degree(table):
            return jnp.pad(table, even).reshape(order_count // 8, slots, lat_total * 8)

        fwd_rows = by_degree(fwd_masked.transpose(0, 3, 2, 1))
        inv_rows = by_degree(inv_masked.transpose(0, 2, 3, 1))

    spectra = lax.all_gather(spectra, "wide", axis=0, tiled=False)
    grid_coef = spectral_forward(spectra, fwd_rows, inv_rows, folded, lat_dev, channels)
    grid_coef = lax.psum_scatter(grid_coef, "wide", scatter_dimension=0, tiled=True)
    grid_coef = grid_coef.reshape(lat_dev, order_count, 2, width)

    encoded = dot("caj,ck->ajk", fields, io_weight[0]) + enc_bias
    mixed_in = encoded + dot("aspc,psj->ajc", grid_coef, inverse)
    hidden_pre = dot("ajk,kh->ajh", mixed_in, mlp_weight[0]) + hidden_bias
    hidden_act, smooth_back = jax.vjp(smooth, hidden_pre)
    latent = mixed_in + dot("ajh,kh->ajk", hidden_act, mlp_weight[1]) + mlp_bias
    predicted = dot("ajk,ck->caj", latent, io_weight[1]) + out_bias[:, None, None]
    misfit = predicted - truth
    pixel_weight = pixel_weights(land_mask, missing_mask[0], position * lat_dev, lat_total, channels)
    count_local = jnp.sum(pixel_weight)
    weighted = pixel_weight * misfit
    loss_local = jnp.sum(weighted * misfit)
    pred_grad = weighted * (2.0 / entries)
    out_bias_grad = jnp.sum(pred_grad, axis=(1, 2))
    decoder_grad = dot("caj,ajk->ck", pred_grad, latent)
    latent_grad = dot("caj,ck->ajk", pred_grad, io_weight[1])
    mlp_bias_grad = jnp.sum(latent_grad, axis=(0, 1))
    down_grad = dot("ajk,ajh->kh", latent_grad, hidden_act)
    act_grad = dot("ajk,kh->ajh", latent_grad, mlp_weight[1])
    pre_grad = smooth_back(act_grad)[0]
    hidden_bias_grad = jnp.sum(pre_grad, axis=(0, 1))
    up_grad = dot("ajk,ajh->kh", mixed_in, pre_grad)
    mixed_grad = latent_grad + dot("ajh,kh->ajk", pre_grad, mlp_weight[0])

    grid_grad = dot("ajc,psj->aspc", mixed_grad, inverse).reshape(lat_dev, order_count, 2 * width)
    grid_grad = lax.all_gather(grid_grad, "wide", axis=0, tiled=True)
    direct = dot("caj,ajk->ck", fields, mixed_grad)
    direct_bias = jnp.sum(mixed_grad, axis=(0, 1))
    small = [direct_bias, hidden_bias_grad, mlp_bias_grad, out_bias_grad, loss_local[None], count_local[None]]
    small = jnp.concatenate(small)
    small_count = small.shape[0]
    flat = [up_grad.reshape(-1, width), down_grad.reshape(-1, width), decoder_grad, direct]
    flat.append(jnp.pad(small, (0, -small_count % width)).reshape(-1, width))
    flat = jnp.concatenate(flat, axis=0)
    flat = all_sum(jnp.pad(flat, ((0, -flat.shape[0] % 32), (0, 0))))
    grid_grad, flat = lax.optimization_barrier((grid_grad, flat))
    thin = spectral_backward(
        grid_grad, spectra, fwd_rows, inv_rows, degree_slots, thin_count, channels
    )
    at = 2 * hidden_units
    mlp_grad = flat[:at].reshape(2, width, hidden_units)
    decoder_grad = flat[at : at + channels]
    direct = flat[at + channels : at + 2 * channels]
    small = flat[at + 2 * channels :].reshape(-1)[:small_count]
    encoder_grad = all_sum(dot("tpck,tpdk->cd", thin[:degree_slots], spectral_weight))
    gram = jnp.einsum("ck,dk->cd", encoder, encoder, precision=lax.Precision.HIGHEST)
    size, first_steps, _ = adam_split(degree_slots)
    pairs = thin.reshape((-1,) + thin.shape[2:])
    parts, spectral_squares = thin_sum(pairs, gram, 4 * size * first_steps)
    io_grad = jnp.stack([direct + encoder_grad[:channels], decoder_grad])
    bias_grad = jnp.concatenate([small[:width] + encoder_grad[channels], small[width:-2]])
    loss_sum, valid_weight = small[-2], small[-1]
    rescale = entries / valid_weight
    squares = (
        spectral_squares
        + jnp.sum(io_grad * io_grad)
        + jnp.sum(mlp_grad * mlp_grad)
        + jnp.sum(bias_grad * bias_grad)
    )
    grad_norm = jnp.sqrt(squares) * rescale
    factor = rescale * CLIP_LIMIT / jnp.maximum(grad_norm, CLIP_LIMIT)
    spectral = ()
    weights = (spectral_weight, spectral_first, spectral_second)
    for half in range(2):
        one, two = (part[half].reshape((-1, 2) + thin.shape[2:]) for part in parts)
        low_one, low_two = ((part[2] if half == 0 else jnp.logical_not(part[2])) for part in parts)
        spectral = spectral_adam(factor[None], encoder, one, two, low_one, low_two, weights, spectral)
    spectral_new, spectral_first_new, spectral_second_new, spectral_low = spectral
    io_new, io_first_new, io_second_new = adam_step(
        io_weight, io_first, io_second, io_grad * factor, WEIGHT_DECAY
    )
    mlp_new, mlp_first_new, mlp_second_new = adam_step(
        mlp_weight, mlp_first, mlp_second, mlp_grad * factor, WEIGHT_DECAY
    )
    bias_new, bias_first_new, bias_second_new = adam_step(
        biases, bias_first, bias_second, bias_grad * factor, 0.0
    )
    return (
        loss_sum,
        valid_weight,
        grad_norm,
        spectral_new,
        spectral_first_new,
        spectral_second_new,
        spectral_low,
        io_new,
        io_first_new,
        io_second_new,
        io_new.astype(jnp.bfloat16),
        mlp_new,
        mlp_first_new,
        mlp_second_new,
        mlp_new.astype(jnp.bfloat16),
        bias_new,
        bias_first_new,
        bias_second_new,
        bias_new.astype(jnp.bfloat16),
    )


def solution(mesh):
    wide4 = P("wide", None, None, None)
    in_specs = (
        P("dp", None, "wide", None),
        P("dp", None, "wide", None),
        P("wide", None),
        P("dp", "wide", None),
        P(),
        P(),
        P("wide", None, None),
        P("wide", None, None),
        wide4,
        wide4,
        wide4,
    ) + (P(),) * 9
    out_specs = (P(),) * 3 + (wide4,) * 4 + (P(),) * 12
    return jax.shard_map(body, mesh=mesh, in_specs=in_specs, out_specs=out_specs, check_vma=False)
```
